256 devices in a mesh: gx: 8 (over z_hi, x), gy: 8 (over z_lo, core), gz: 4 (over y).
Axes of the slice: x: 4, y: 4, z: 8 (z_hi: 2, z_lo: 4; z = z_hi * 4 + z_lo), core: 2. Of those that a mesh axis runs over, the one named last changes fastest.
Arguments:
- tokens: bfloat16 [1024, 6144], P('gx', ('gz', 'gy')), may hold values from -6 to 6
- w_in: bfloat16 [6144, 24576], P(('gz', 'gx'), 'gy'), may hold values from -0.078125 to 0.078125
- w_out: bfloat16 [24576, 6144], P(('gy', 'gx'), 'gz'), may hold values from -0.0390625 to 0.0390625
- cotangent: bfloat16 [1024, 6144], P('gx', ('gz', 'gy')), may hold values from -1.5 to 1.5
Outputs:
- output: bfloat16 [1024, 6144], P('gx', ('gz', 'gy'))
- grad_tokens: bfloat16 [1024, 6144], P('gx', ('gz', 'gy'))
- grad_in: bfloat16 [6144, 24576], P(('gz', 'gx'), 'gy')
- grad_out: bfloat16 [24576, 6144], P(('gy', 'gx'), 'gz')
The draws below stay inside these ranges and needn't reach their ends.
All inputs are finite; a program needn't handle non-finite values.
Results may differ from the reference program's by a relative error of at most 0.019.
Values may be sent and summed in bfloat16 or wider, within the bound.
A program may use at most 128 MiB of HBM per device.

```python
import jax
import jax.numpy as jnp
from jax import lax

D = 6144
FF = 24576
TOKENS = 1024


def shard_levels(key, shape, cuts, least, high):
    level, own = 1.0, jax.random.fold_in(key, 6)
    for dim, parts in cuts:
        heights = jnp.exp(jax.random.uniform(jax.random.fold_in(own, dim), (parts,), jnp.float32, least / len(cuts), high / len(cuts)))
        level = level * jnp.repeat(heights, shape[dim] // parts).reshape([-1 if axis == dim else 1 for axis in range(len(shape))])
    return level


def normal_values(key, dims, width, bound, split=(), dtype=jnp.bfloat16):
    gain = shard_levels(key, dims, split, -0.22, 0.18) if split else 1.0
    result = jax.random.normal(key, dims, jnp.float32) * width * gain
    return jnp.minimum(jnp.maximum(result, -bound), bound).astype(dtype)


def setup_inputs(seed: int = 0) -> dict:
    keys = jax.random.split(jax.random.key(seed), 5)
    tokens = normal_values(keys[0], (TOKENS, D), 1.0, 6.0, ((0, 8), (1, 32)))
    w_in = normal_values(keys[1], (D, FF), D ** -0.5, 0.078125, ((0, 32), (1, 8)))
    w_out = normal_values(keys[2], (FF, D), FF ** -0.5, 0.0390625, ((0, 64), (1, 4)))
    cotangent = normal_values(keys[3], (TOKENS, D), 0.25, 1.5, ((0, 8), (1, 32)))
    return dict(tokens=tokens, w_in=w_in, w_out=w_out, cotangent=cotangent)


gelu_scale = 0.7978845608


def gelu_value(pre):
    inner = gelu_scale * (pre + 0.044715 * pre * pre * pre)
    return 0.5 * pre * (1.0 + jnp.tanh(inner))


def gelu_slope(pre):
    inner = gelu_scale * (pre + 0.044715 * pre * pre * pre)
    tangent = jnp.tanh(inner)
    return 0.5 * (1.0 + tangent) + 0.5 * pre * (1.0 - tangent * tangent) * gelu_scale * (1.0 + 0.134145 * pre * pre)


def contract(left, right, left_dim, right_dim):
    return lax.dot_general(left, right, (((left_dim,), (right_dim,)), ((), ())), preferred_element_type=jnp.float32)


def reference(tokens, w_in, w_out, cotangent):
    pre = jnp.dot(tokens, w_in, preferred_element_type=jnp.float32)
    act = gelu_value(pre).astype(jnp.bfloat16)
    output = jnp.dot(act, w_out, preferred_element_type=jnp.float32).astype(jnp.bfloat16)
    back = contract(cotangent, w_out, 1, 1)
    grad_pre = (back * gelu_slope(pre)).astype(jnp.bfloat16)
    grad_tokens = contract(grad_pre, w_in, 1, 1).astype(jnp.bfloat16)
    grad_in = contract(tokens, grad_pre, 0, 0).astype(jnp.bfloat16)
    grad_out = contract(act, cotangent, 0, 0).astype(jnp.bfloat16)
    return (output, grad_tokens, grad_in, grad_out)
```

```python
import functools

import jax
import jax.numpy as jnp
from jax import lax
from jax.experimental import pallas as pl
from jax.experimental.pallas import tpu as pltpu
from jax.sharding import PartitionSpec as P

MESH = pl.DeviceIdType.MESH
gelu_scale = 0.7978845608
bf16, f32 = jnp.bfloat16, jnp.float32


def contract(left, right, left_dim, right_dim):
    return lax.dot_general(
        left, right, (((left_dim,), (right_dim,)), ((), ())), preferred_element_type=f32
    )


def kernel(
    tok, w_in, w_out, cot, out, grad_tok, grad_in, grad_out,
    tok_sib, cot_sib, tok_piece, cot_piece, tok_all, cot_all, w_mine,
    pre_send, pre_recv, pre_sum, half_send, half_recv,
    back_send, back_recv, back_sum, act, gp,
    out_sib_send, out_sib_recv, out_own, out_x_send, out_x_recv, out_x_sum, out_z_send, out_z_recv, out_fin,
    gt_sib_send, gt_sib_recv, gt_own, gt_x_send, gt_x_recv, gt_x_sum, gt_z_send, gt_z_recv, gt_fin,
    gi_send, local_sem,
    in_ss, in_rs, w_ss, w_rs, tz_ss, tz_rs, cz_ss, cz_rs, tx_ss, tx_rs, cx_ss, cx_rs, tsib_ss, tsib_rs, csib_ss, csib_rs,
    pre_ss, pre_rs, half_ss, half_rs, back_ss, back_rs, act_ss, act_rs, gp_ss, gp_rs,
    osib_ss, osib_rs, ox_ss, ox_rs, oz_ss, oz_rs, of_ss, of_rs,
    gsib_ss, gsib_rs, gx_ss, gx_rs, gz_ss, gz_rs, gf_ss, gf_rs, gi_ss, gi_rs,
):
    ax, ay, y = lax.axis_index("gx"), lax.axis_index("gy"), lax.axis_index("gz")
    zh, x = ax // 4, lax.rem(ax, 4)
    zl, c = ay // 2, lax.rem(ay, 2)
    z = zh * 4 + zl
    oc, oh = 1 - c, 1 - zh

    def dev(x_, y_, z_, c_):
        return (z_ // 4 * 4 + x_, lax.rem(z_, 4) * 2 + c_, y_)

    def at_x(d):
        return dev(lax.rem(x + d, 4), y, z, c)

    def at_y(d):
        return dev(x, lax.rem(y + d, 4), z, c)

    def at_z(d):
        return dev(x, y, lax.rem(z + d, 8), c)

    sib = dev(x, y, z, oc)
    started = []

    def copy(src, dst, ss, rs, to):
        return pltpu.make_async_remote_copy(
            src_ref=src, dst_ref=dst, send_sem=ss, recv_sem=rs, device_id=to, device_id_type=MESH
        )

    def send(src, dst, ss, rs, to):
        one = copy(src, dst, ss, rs, to)
        one.start()
        started.append(one)
        return one

    barrier = pltpu.get_barrier_semaphore()
    peers = [at_x(d) for d in (1, 2, 3)] + [at_y(d) for d in (1, 2, 3)] + [at_z(d) for d in range(1, 8)] + [sib]
    for peer in peers:
        pl.semaphore_signal(barrier, inc=1, device_id=peer, device_id_type=MESH)
    pl.semaphore_wait(barrier, len(peers))

    other_rows = pl.ds(pl.multiple_of(oc * 64, 64), 64)
    my_rows = pl.ds(pl.multiple_of(c * 64, 64), 64)
    t_in = send(tok.at[other_rows], tok_sib, in_ss.at[0], in_rs.at[0], sib)
    c_in = send(cot.at[other_rows], cot_sib, in_ss.at[1], in_rs.at[1], sib)

    def w_cols(block, x_):
        return pl.ds(pl.multiple_of((block * 4 + x_) * 384, 384), 384)

    w_rows = pl.ds(pl.multiple_of(x * 192, 192), 192)
    w_copies = []
    for d in (2, 1, 3):
        to = lax.rem(x + d, 4)
        for b in range(2):
            w_copies.append(
                send(
                    w_in.at[:, w_cols(b, to)], w_mine.at[w_rows, pl.ds(b * 384, 384)],
                    w_ss.at[d - 1, b], w_rs.at[d - 1, b], at_x(d),
                )
            )
    for b in range(2):
        w_mine[w_rows, pl.ds(b * 384, 384)] = w_in[:, w_cols(b, x)]

    row = lax.broadcasted_iota(jnp.int32, (192, 384), 0)
    col = lax.broadcasted_iota(jnp.int32, (192, 384), 1)
    put_own = jnp.where(col == row + 192 * c, 1.0, 0.0).astype(bf16)
    put_sib = jnp.where(col == row + 192 * oc, 1.0, 0.0).astype(bf16)
    t_in.wait_recv()
    tok_piece[...] = (contract(tok[my_rows, :], put_own, 1, 0) + contract(tok_sib[...], put_sib, 1, 0)).astype(bf16)

    half = zl // 2
    t_rows = pl.ds(pl.multiple_of(c * 512 + x * 128 + zh * 64, 64), 64)
    t_cols = pl.ds(pl.multiple_of(lax.rem(zl, 2) * 384, 384), 384)
    t_slot = zh * 2 + lax.rem(zl, 2)
    t_out = []
    for j in range(4):
        mine = jnp.logical_and(half == zh, zl == j)
        one = copy(
            tok_piece, tok_all.at[t_rows, t_cols], tz_ss.at[j], tz_rs.at[t_slot], dev(x, y, half * 4 + j, c)
        )
        t_out.append((mine, one))

        @pl.when(jnp.logical_not(mine))
        def _():
            one.start()

    @pl.when(half == zh)
    def _():
        tok_all[t_rows, t_cols] = tok_piece[...]

    c_in.wait_recv()
    cot_piece[...] = (contract(cot[my_rows, :], put_own, 1, 0) + contract(cot_sib[...], put_sib, 1, 0)).astype(bf16)
    c_cols = pl.ds(pl.multiple_of(zl * 384, 384), 384)
    cz = [
        send(cot_piece, cot_all.at[t_rows, c_cols], cz_ss.at[d - 1], cz_rs.at[d - 1], at_z(d))
        for d in (4, 3, 5, 2, 6, 1, 7)
    ]
    cot_all[t_rows, c_cols] = cot_piece[...]

    for s in range(2):
        for l in range(2):
            mine = jnp.logical_and(zh == s, zl == 2 * zh + l)
            one = copy(tok_piece, tok_all.at[t_rows, t_cols], tz_ss.at[0], tz_rs.at[s * 2 + l], sib)

            @pl.when(jnp.logical_not(mine))
            def _():
                one.wait_recv()

    def x_rows(d):
        return pl.ds(pl.multiple_of(c * 512 + lax.rem(x + d, 4) * 128, 128), 128)

    def gather_x(whole, ss, rs):
        return {d: send(whole.at[x_rows(0)], whole.at[x_rows(0)], ss.at[d - 1], rs.at[d - 1], at_x(d)) for d in (2, 1, 3)}

    def to_sibling(whole, ss, rs, d):
        return send(whole.at[x_rows(d)], whole.at[x_rows(d)], ss.at[d], rs.at[d], sib)

    tx = gather_x(tok_all, tx_ss, tx_rs)
    t_sib = [to_sibling(tok_all, tsib_ss, tsib_rs, 0)]
    for one in cz:
        one.wait_recv()
    cx = gather_x(cot_all, cx_ss, cx_rs)
    c_sib = [to_sibling(cot_all, csib_ss, csib_rs, 0)]
    for d in (1, 3, 2):
        tx[d].wait_recv()
        t_sib.append(to_sibling(tok_all, tsib_ss, tsib_rs, 4 - d))
    for one in w_copies:
        one.wait_recv()
    for one in t_sib:
        one.wait_recv()

    def y_rows(d):
        return pl.ds(pl.multiple_of(lax.rem(y + d, 4) * 256, 256), 256)

    def block_cols(b):
        return pl.ds(pl.multiple_of(b * 384, 384), 384)

    pre = []
    for i, b in enumerate((oh, zh)):
        for d in (2, 1, 3):
            pre_send[i, d - 1] = contract(tok_all[y_rows(d), :], w_mine[:, block_cols(b)], 1, 0).astype(bf16)
            pre.append(
                send(pre_send.at[i, d - 1], pre_recv.at[i, d - 1], pre_ss.at[i, d - 1], pre_rs.at[i, d - 1], at_y(d))
            )
        pre_sum[i] = contract(tok_all[y_rows(0), :], w_mine[:, block_cols(b)], 1, 0)

    for one in pre[:3]:
        one.wait_recv()
    half_send[...] = (
        pre_sum[0] + pre_recv[0, 0].astype(f32) + pre_recv[0, 1].astype(f32) + pre_recv[0, 2].astype(f32)
    ).astype(bf16)
    across = send(half_send, half_recv, half_ss, half_rs, at_z(4))

    for d in (1, 3, 2):
        cx[d].wait_recv()
        c_sib.append(to_sibling(cot_all, csib_ss, csib_rs, 4 - d))
    for one in c_sib:
        one.wait_recv()
    back = []
    for d in (2, 1, 3):
        back_send[d - 1] = contract(cot_all[y_rows(d), :], w_out[...], 1, 1).astype(bf16)
        back.append(send(back_send.at[d - 1], back_recv.at[d - 1], back_ss.at[d - 1], back_rs.at[d - 1], at_y(d)))
    back_sum[...] = contract(cot_all[y_rows(0), :], w_out[...], 1, 1)

    for one in pre[3:]:
        one.wait_recv()
    pre_sum[1] = pre_sum[1] + pre_recv[1, 0].astype(f32) + pre_recv[1, 1].astype(f32) + pre_recv[1, 2].astype(f32)
    across.wait_recv()
    h = pre_sum[1] + half_recv[...].astype(f32)
    t = jnp.tanh(gelu_scale * (h + 0.044715 * h * h * h))
    act[y_rows(0), :] = (0.5 * h * (1.0 + t)).astype(bf16)
    pre_sum[0] = 0.5 * (1.0 + t) + 0.5 * h * (1.0 - t * t) * gelu_scale * (1.0 + 0.134145 * h * h)
    acts = [
        send(act.at[y_rows(0)], act.at[y_rows(0)], act_ss.at[d - 1], act_rs.at[d - 1], at_y(d)) for d in (2, 1, 3)
    ]

    for one in back:
        one.wait_recv()
    total = back_sum[...] + back_recv[0].astype(f32) + back_recv[1].astype(f32) + back_recv[2].astype(f32)
    gp[y_rows(0), block_cols(zh)] = (total * pre_sum[0]).astype(bf16)

    def gp_block(b):
        return gp.at[y_rows(0), block_cols(b)]

    gp_half = send(gp_block(zh), gp_block(zh), gp_ss.at[2, 0], gp_rs.at[2, 0], at_z(4))
    gps = [
        send(gp_block(zh), gp_block(zh), gp_ss.at[0, d - 1], gp_rs.at[0, d - 1], at_y(d)) for d in (2, 1, 3)
    ]

    def core_rows(core, i):
        return pl.ds(pl.multiple_of(core * 512 + i * 256, 256), 256)

    def scatter_sib(part, send_ref, recv_ref, own, ss, rs):
        for i in range(2):
            send_ref[pl.ds(i * 256, 256), :] = part(core_rows(oc, i)).astype(bf16)
        one = send(send_ref, recv_ref, ss, rs, sib)
        for i in range(2):
            own[pl.ds(i * 256, 256), :] = part(core_rows(c, i))
        return one

    def scatter_x(recv_ref, own, x_send, x_recv, ss, rs):
        copies = []
        for d in (2, 1, 3, 0):
            rows = pl.ds(pl.multiple_of(lax.rem(x + d, 4) * 128, 128), 128)
            both = own[rows, :] + recv_ref[rows, :].astype(f32)
            if d:
                x_send[d - 1] = both.astype(bf16)
                copies.append(send(x_send.at[d - 1], x_recv.at[d - 1], ss.at[d - 1], rs.at[d - 1], at_x(d)))
        return copies, both

    for one in acts:
        one.wait_recv()
    o_sib = scatter_sib(lambda rows: contract(act[rows, :], w_out[...], 1, 0), out_sib_send, out_sib_recv, out_own, osib_ss, osib_rs)
    o_sib.wait_recv()
    ox, mine = scatter_x(out_sib_recv, out_own, out_x_send, out_x_recv, ox_ss, ox_rs)
    out_x_sum[...] = mine

    gp_half.wait_recv()
    gps += [
        send(gp_block(oh), gp_block(oh), gp_ss.at[1, d - 1], gp_rs.at[1, d - 1], at_y(d)) for d in (2, 1, 3)
    ]

    for n in range(4):
        cols = pl.ds(n * 384, 384)
        grad_out[:, cols] = contract(act[...], cot_all[:, cols], 0, 0).astype(bf16)

    for one in ox:
        one.wait_recv()
    out_x_sum[...] = out_x_sum[...] + out_x_recv[0].astype(f32) + out_x_recv[1].astype(f32) + out_x_recv[2].astype(f32)
    out_z_send[...] = out_x_sum[...].astype(bf16)

    def z_part(ref, z_):
        rows = pl.ds(pl.multiple_of(z_ // 4 * 64, 64), 64)
        return ref.at[rows, pl.ds(pl.multiple_of(lax.rem(z_, 4) * 384, 384), 384)]

    oz = [
        send(z_part(out_z_send, lax.rem(z + d, 8)), out_z_recv.at[d - 1], oz_ss.at[d - 1], oz_rs.at[d - 1], at_z(d))
        for d in (4, 3, 5, 2, 6, 1, 7)
    ]

    for one in gps:
        one.wait_recv()
    g_sib = scatter_sib(lambda rows: contract(gp[rows, :], w_mine[...], 1, 1), gt_sib_send, gt_sib_recv, gt_own, gsib_ss, gsib_rs)
    g_sib.wait_recv()
    gx, mine = scatter_x(gt_sib_recv, gt_own, gt_x_send, gt_x_recv, gx_ss, gx_rs)
    gt_x_sum[...] = mine

    for p in range(2):
        rows = pl.ds(p * 384, 384)
        gi_send[rows, :] = contract(tok_all[:, rows], gp[...], 0, 0).astype(bf16)
    gi = []
    for d in (2, 1, 3):
        rows = pl.ds(pl.multiple_of(lax.rem(x + d, 4) * 192, 192), 192)
        for b in range(2):
            gi.append(
                send(
                    gi_send.at[rows, pl.ds(b * 384, 384)], grad_in.at[:, w_cols(b, x)],
                    gi_ss.at[d - 1, b], gi_rs.at[d - 1, b], at_x(d),
                )
            )
    for b in range(2):
        grad_in[:, w_cols(b, x)] = gi_send[w_rows, pl.ds(b * 384, 384)]

    for one in oz:
        one.wait_recv()
    total = z_part(out_x_sum, z)[...]
    for i in range(7):
        total = total + out_z_recv[i].astype(f32)
    out_fin[my_rows, :] = total.astype(bf16)
    o_fin = send(out_fin.at[my_rows], out_fin.at[my_rows], of_ss, of_rs, sib)

    for one in gx:
        one.wait_recv()
    gt_x_sum[...] = gt_x_sum[...] + gt_x_recv[0].astype(f32) + gt_x_recv[1].astype(f32) + gt_x_recv[2].astype(f32)
    gt_z_send[...] = gt_x_sum[...].astype(bf16)
    g_out = []
    for s in range(2):
        for l in range(2):
            to = s * 4 + 2 * zh + l
            mine = jnp.logical_and(zh == s, zl == 2 * zh + l)
            part = gt_z_send.at[pl.ds(s * 64, 64), pl.ds(l * 384, 384)]
            one = copy(part, gt_z_recv.at[zl], gz_ss.at[s * 2 + l], gz_rs.at[zl], dev(x, y, to, c))
            g_out.append((mine, one))

            @pl.when(jnp.logical_not(mine))
            def _():
                one.start()

            @pl.when(mine)
            def _():
                gt_z_recv[zl] = part[...]

    for j in range(4):
        mine = jnp.logical_and(half == zh, zl == j)
        one = copy(gt_z_send.at[pl.ds(0, 64), pl.ds(0, 384)], gt_z_recv.at[j], gz_ss.at[0], gz_rs.at[j], sib)

        @pl.when(jnp.logical_not(mine))
        def _():
            one.wait_recv()

    total = gt_z_recv[0].astype(f32)
    for j in range(1, 4):
        total = total + gt_z_recv[j].astype(f32)
    gt_fin[my_rows, :] = total.astype(bf16)
    g_fin = send(gt_fin.at[my_rows], gt_fin.at[my_rows], gf_ss, gf_rs, sib)

    row = lax.broadcasted_iota(jnp.int32, (384, 192), 0)
    col = lax.broadcasted_iota(jnp.int32, (384, 192), 1)
    take = jnp.where(row == col + 192 * c, 1.0, 0.0).astype(bf16)
    o_fin.wait_recv()
    out[...] = contract(out_fin[...], take, 1, 0).astype(bf16)
    g_fin.wait_recv()
    grad_tok[...] = contract(gt_fin[...], take, 1, 0).astype(bf16)
    for one in gi:
        one.wait_recv()
    for one in started:
        one.wait_send()
    for mine, one in t_out + g_out:

        @pl.when(jnp.logical_not(mine))
        def _():
            one.wait_send()


def on_device(tokens, w_in, w_out, cotangent):
    def buf(*shape, dtype=bf16):
        return pltpu.VMEM(shape, dtype)

    def sems(*shape):
        return pltpu.SemaphoreType.DMA(shape)

    dma = pltpu.SemaphoreType.DMA
    scratch = [
        buf(64, 192), buf(64, 192), buf(64, 384), buf(64, 384), buf(1024, 768), buf(1024, 1536), buf(768, 768),
        buf(2, 3, 256, 384), buf(2, 3, 256, 384), buf(2, 256, 384, dtype=f32), buf(256, 384), buf(256, 384),
        buf(3, 256, 384), buf(3, 256, 384), buf(256, 384, dtype=f32), buf(1024, 384), buf(1024, 768),
    ]
    for wide, parts in ((1536, 7), (768, 4)):
        scratch += [
            buf(512, wide), buf(512, wide), buf(512, wide, dtype=f32), buf(3, 128, wide), buf(3, 128, wide),
            buf(128, wide, dtype=f32), buf(128, wide), buf(parts, 64, 384), buf(128, 384),
        ]
    scratch += [buf(768, 768), dma]
    for shape in (
        (2,), (3, 2), (4,), (7,), (3,), (3,), (4,), (4,), (2, 3), (), (3,), (3,), (3, 3),
        (), (3,), (7,), (), (), (3,), (4,), (), (3, 2),
    ):
        scratch += [sems(*shape) if shape else dma] * 2
    shape = jax.ShapeDtypeStruct
    vmem = pl.BlockSpec(memory_space=pltpu.VMEM)
    return pl.pallas_call(
        kernel,
        out_shape=(shape((128, 192), bf16), shape((128, 192), bf16), shape((192, 3072), bf16), shape((384, 1536), bf16)),
        in_specs=[vmem] * 4,
        out_specs=[vmem] * 4,
        scratch_shapes=scratch,
        compiler_params=pltpu.CompilerParams(
            collective_id=0, has_side_effects=True, vmem_limit_bytes=58 * 1024 * 1024
        ),
        cost_estimate=pl.CostEstimate(flops=7_250_000_000, bytes_accessed=5_000_000, transcendentals=100_000),
    )(tokens, w_in, w_out, cotangent)


def solution(mesh):
    specs = (P("gx", ("gz", "gy")), P(("gz", "gx"), "gy"), P(("gy", "gx"), "gz"))
    return jax.shard_map(
        on_device,
        mesh=mesh,
        in_specs=(specs[0], specs[1], specs[2], specs[0]),
        out_specs=(specs[0], specs[0], specs[1], specs[2]),
        check_vma=False,
    )
```

```python
import types

import jax
import jax.numpy as jnp
from jax import lax
from jax.experimental import pallas as pl
from jax.experimental.pallas import tpu as pltpu
from jax.sharding import PartitionSpec as P

MESH = pl.DeviceIdType.MESH
gelu_scale = 0.7978845608
bf16, f32 = jnp.bfloat16, jnp.float32


def contract(left, right, left_dim, right_dim):
    return lax.dot_general(
        left, right, (((left_dim,), (right_dim,)), ((), ())), preferred_element_type=f32
    )


def buffers():
    return dict(
        tok=((192, 128), bf16), cot=((192, 128), bf16), w_out=((384, 1536), bf16), grad_out=((384, 1536), bf16),
        tok_sib=((192, 128), bf16), cot_sib=((192, 128), bf16),
        tok_chip=((2, 4, 16, 384), bf16), cot_chip=((2, 4, 16, 384), bf16),
        tok_all=((4, 4, 64, 768), bf16), cot_all=((4, 4, 64, 1536), bf16), w_mine=((768, 768), bf16),
        pre_part=((2, 4, 4, 64, 384), f32), pre_send=((2, 4, 3, 64, 384), bf16),
        pre_fwd=((2, 4, 64, 384), bf16), pre_recv=((2, 4, 2, 64, 384), bf16),
        half_send=((4, 64, 384), bf16), half_recv=((4, 64, 384), bf16),
        back_part=((4, 256, 384), f32), back_send=((3, 256, 384), bf16),
        back_fwd=((2, 128, 384), bf16), back_recv=((2, 256, 384), bf16), slope=((256, 384), f32),
        act=((4, 256, 384), bf16), gp=((4, 256, 768), bf16),
        o_part=((4, 4, 64, 1536), f32), o_sib_send=((4, 4, 32, 1536), bf16), o_sib_recv=((4, 4, 32, 1536), bf16),
        o_own=((4, 4, 32, 1536), f32), o_ring_send=((4, 2, 4, 4, 16, 384), bf16), o_ring_recv=((4, 2, 4, 4, 16, 384), bf16),
        o_x_send=((4, 4, 16, 384), bf16), o_x_recv=((4, 3, 16, 384), bf16), o_x_own=((4, 4, 16, 384), f32),
        o_fin=((2, 4, 16, 384), bf16),
        g_part=((4, 4, 64, 768), f32), g_sib_send=((4, 4, 32, 768), bf16), g_sib_recv=((4, 4, 32, 768), bf16),
        g_own=((4, 4, 32, 768), f32), g_x_send=((4, 3, 32, 768), bf16), g_x_recv=((4, 3, 32, 768), bf16),
        g_z_send=((4, 32, 768), bf16), g_z_recv=((4, 4, 16, 384), bf16),
        g_fin=((2, 4, 16, 384), bf16), gi_send=((768, 768), bf16),
    )


def semaphores():
    return dict(
        inp=(2,), w=(3, 2), tz=(4,), cx=(3,), cz=(2, 4, 2), csib=(8, 2), tx=(3,), tsib=(4,),
        pre=(2, 4, 3), half=(4,), back=(6,), act=(4,), gp=(2, 4), gph=(4,),
        osib=(4,), oring=(4, 2, 4), ox=(4, 3), ofin=(1,),
        gsib=(4,), gx=(4, 3), gz=(4, 4), gfin=(1,), gi=(2, 3),
    )


def kernel(*refs):
    tok_hbm, w_in, w_out_hbm, cot_hbm, out, grad_tok, grad_in, grad_out_hbm = refs[:8]
    bufs = buffers()
    r = types.SimpleNamespace(**dict(zip(bufs, refs[8:])))
    rest = refs[8 + len(bufs):]
    local = rest[-1]
    sem = types.SimpleNamespace(**{name: rest[2 * i : 2 * i + 2] for i, name in enumerate(semaphores())})
    tok_all, cot_all, w_mine, act, gp = r.tok_all, r.cot_all, r.w_mine, r.act, r.gp

    ax, ay, y = lax.axis_index("gx"), lax.axis_index("gy"), lax.axis_index("gz")
    zh, x = ax // 4, lax.rem(ax, 4)
    zl, c = ay // 2, lax.rem(ay, 2)
    z = zh * 4 + zl
    oc, oh = 1 - c, 1 - zh

    def dev(x_, y_, z_, c_):
        return (z_ // 4 * 4 + x_, lax.rem(z_, 4) * 2 + c_, y_)

    def mod(v, d, n):
        return lax.rem(v + d, n)

    def at_x(d):
        return dev(mod(x, d, 4), y, z, c)

    def at_y(d):
        return dev(x, mod(y, d, 4), z, c)

    def at_z(d):
        return dev(x, y, mod(z, d, 8), c)

    sib = dev(x, y, z, oc)
    started, coming, maybe = [], [], []

    def copy(src, dst, pair, index, to, from_index=None):
        ss, rs = pair
        return pltpu.make_async_remote_copy(
            src_ref=src, dst_ref=dst, send_sem=ss.at[index], recv_sem=rs.at[index if from_index is None else from_index],
            device_id=to, device_id_type=MESH,
        )

    def send(src, dst, pair, index, to):
        one = copy(src, dst, pair, index, to)
        one.start()
        started.append(one)
        coming.append(one)
        return one

    def recv(*copies):
        for one in copies:
            one.wait_recv()
            coming[:] = [other for other in coming if other is not one]

    def send_unless(mine, one):
        maybe.append((mine, one))

        @pl.when(jnp.logical_not(mine))
        def _():
            one.start()

    def recv_unless(mine, one):
        @pl.when(jnp.logical_not(mine))
        def _():
            one.wait_recv()

    def span(i, n):
        return pl.ds(i * n if isinstance(i, int) else pl.multiple_of(i * n, n), n)

    tok, cot, w_out, grad_out = r.tok, r.cot, r.w_out, r.grad_out
    loads = []

    def load(src, dst):
        one = pltpu.make_async_copy(src, dst, local.at[len(loads)])
        one.start()
        loads.append(one)
        return one

    t_load, c_load = load(tok_hbm, tok), load(cot_hbm, cot)

    barrier = pltpu.get_barrier_semaphore()
    peers = [at_x(d) for d in (1, 2, 3)] + [at_y(d) for d in (1, 2, 3)] + [at_z(d) for d in range(1, 8)] + [sib]
    for peer in peers:
        pl.semaphore_signal(barrier, inc=1, device_id=peer, device_id_type=MESH)
    pl.semaphore_wait(barrier, len(peers))

    t_load.wait()
    c_load.wait()
    t_in = send(tok, r.tok_sib, sem.inp, 0, sib)
    c_in = send(cot, r.cot_sib, sem.inp, 1, sib)

    def w_cols(block, x_):
        return span(block * 4 + x_, 384)

    w_copies = [
        send(w_in.at[:, w_cols(b, mod(x, d, 4))], w_mine.at[span(x, 192), span(b, 384)], sem.w, (d - 1, b), at_x(d))
        for d in (2, 1, 3)
        for b in range(2)
    ]

    w_loads = [load(w_in.at[:, w_cols(b, x)], w_mine.at[span(x, 192), span(b, 384)]) for b in range(2)]
    w_out_load = load(w_out_hbm, w_out)

    row = lax.broadcasted_iota(jnp.int32, (192, 384), 0)
    col = lax.broadcasted_iota(jnp.int32, (192, 384), 1)
    put_own = jnp.where(col == row + 192 * c, 1.0, 0.0).astype(bf16)
    put_sib = jnp.where(col == row + 192 * oc, 1.0, 0.0).astype(bf16)

    def chip(own, other):
        both = contract(own[...], put_own, 0, 0) + contract(other[...], put_sib, 0, 0)
        return both.astype(bf16).reshape(2, 4, 16, 384)

    recv(t_in)
    r.tok_chip[...] = chip(tok, r.tok_sib)

    half, l_mine = zl // 2, lax.rem(zl, 2)
    my16 = span(c * 2 + zh, 16)
    t_piece, t_place = r.tok_chip.at[c], tok_all.at[:, x, my16, span(l_mine, 384)]
    for j in (0, 1, 2, 3):
        send_unless(
            jnp.logical_and(half == zh, zl == j),
            copy(t_piece, t_place, sem.tz, (j,), dev(x, y, half * 4 + j, c), (zh * 2 + l_mine,)),
        )

    @pl.when(half == zh)
    def _():
        t_place[...] = t_piece[...]

    recv(c_in)
    r.cot_chip[...] = chip(cot, r.cot_sib)
    c_piece, c_place = r.cot_chip.at[c], cot_all.at[:, x, my16, span(zl, 384)]
    cx = [send(c_piece, c_place, sem.cx, (d - 1,), at_x(d)) for d in (2, 1, 3)]
    c_place[...] = c_piece[...]

    def c_flow():
        c_sib = []

        def block(d, k):
            z_ = mod(z, d + 8, 8)
            return cot_all.at[span(k, 2), :, span(c * 2 + z_ // 4, 16), span(lax.rem(z_, 4), 384)]

        def onward(d, k, way, s):
            return send(block(d, k), block(d, k), sem.cz, (way, s, k), at_z(1 if way == 0 else 7))

        def to_sib(d, k):
            c_sib.append(send(block(d, k), block(d, k), sem.csib, (d % 8, k), sib))

        recv(*cx)
        ring = {}
        for k in range(2):
            for way in range(2):
                ring[way, k] = onward(0, k, way, 0)
        for k in range(2):
            to_sib(0, k)
        yield
        for s in range(1, 4):
            for k in range(2):
                for way in range(2):
                    recv(ring[way, k])
                    d = -s if way == 0 else s
                    if s < 3 or k == way:
                        ring[way, k] = onward(d, k, way, s)
                    to_sib(d, k)
            yield
        for k in range(2):
            recv(ring[k, k])
            to_sib(4, k)
        yield
        recv(*c_sib)
        yield

    c_steps = c_flow()
    next(c_steps)

    for s in range(2):
        for l in range(2):
            recv_unless(
                jnp.logical_and(zh == s, zl == 2 * zh + l), copy(t_piece, t_place, sem.tz, (0,), sib, (s * 2 + l,))
            )

    def t_rows(d):
        return tok_all.at[:, mod(x, d, 4), span(c, 32)]

    tx = {d: send(t_rows(0), t_rows(0), sem.tx, (d - 1,), at_x(d)) for d in (1, 3, 2)}
    t_sib = {0: send(t_rows(0), t_rows(0), sem.tsib, (0,), sib)}

    def t_arrive(d):
        recv(tx[4 - d])
        t_sib[d] = send(t_rows(d), t_rows(d), sem.tsib, (d,), sib)

    steps_x = (0, 1, 3, 2)
    blocks = (oh, zh)
    fwd, direct, joined = {}, {}, {}

    def pre_block(i):
        d = steps_x[i]
        recv(t_sib[d])
        rows = tok_all[:, mod(x, d, 4)].reshape(256, 768)
        near, far = (1, 3) if i % 2 == 0 else (3, 1)
        for b in range(2):
            r.pre_part[b, i] = contract(rows, w_mine[:, span(blocks[b], 384)], 1, 0).reshape(4, 64, 384)
            for j, to in ((0, near), (1, far)):
                whose = 2 if j == 0 else far
                r.pre_send[b, i, j] = r.pre_part[b, i, mod(y, whose, 4)].astype(bf16)
                src = r.pre_send.at[b, i, j]
                if j == 0:
                    fwd[b, i] = send(src, r.pre_fwd.at[b, i], sem.pre, (b, i, 0), at_y(to))
                else:
                    direct[b, i] = send(src, r.pre_recv.at[b, i, 0], sem.pre, (b, i, 1), at_y(to))

    def pre_join(b, i):
        near = 1 if i % 2 == 0 else 3
        recv(fwd[b, i])
        r.pre_send[b, i, 2] = (r.pre_part[b, i, mod(y, near, 4)] + r.pre_fwd[b, i].astype(f32)).astype(bf16)
        joined[b, i] = send(r.pre_send.at[b, i, 2], r.pre_recv.at[b, i, 1], sem.pre, (b, i, 2), at_y(near))

    def pre_total(b, i):
        recv(direct[b, i], joined[b, i])
        return r.pre_part[b, i, y] + r.pre_recv[b, i, 0].astype(f32) + r.pre_recv[b, i, 1].astype(f32)

    across = {}

    def pre_across(i):
        r.half_send[i] = pre_total(0, i).astype(bf16)
        across[i] = send(r.half_send.at[i], r.half_recv.at[i], sem.half, (i,), at_z(4))

    next(c_steps)
    for one in w_loads:
        one.wait()
    recv(*w_copies)
    pre_block(0)
    next(c_steps)
    t_arrive(1)
    t_arrive(3)
    pre_block(1)
    pre_join(0, 0)
    pre_join(1, 0)
    pre_block(2)
    next(c_steps)
    t_arrive(2)
    pre_join(0, 1)
    pre_join(1, 1)
    pre_block(3)
    pre_across(0)
    pre_join(0, 2)
    pre_join(1, 2)
    pre_across(1)
    next(c_steps)
    pre_join(0, 3)
    pre_join(1, 3)
    pre_across(2)
    next(c_steps)

    low, high = span(0, 128), span(1, 128)
    back_part, back_send, back_recv, back_fwd = r.back_part, r.back_send, r.back_recv, r.back_fwd
    w_out_load.wait()
    for d in (2, 1, 3, 0):
        back_part[d] = contract(cot_all[mod(y, d, 4)].reshape(256, 1536), w_out[...], 1, 1)
        if d == 2:
            back_send[1] = back_part[2].astype(bf16)
            b_low = send(back_send.at[1, low], back_fwd.at[0], sem.back, (0,), at_y(1))
            b_high = send(back_send.at[1, high], back_fwd.at[1], sem.back, (1,), at_y(3))
        elif d == 1:
            back_send[0, high] = back_part[1, high].astype(bf16)
            b_direct = [send(back_send.at[0, high], back_recv.at[0, high], sem.back, (2,), at_y(1))]
        elif d == 3:
            back_send[2, low] = back_part[3, low].astype(bf16)
            b_direct.append(send(back_send.at[2, low], back_recv.at[1, low], sem.back, (3,), at_y(3)))
    pre_across(3)
    recv(b_low)
    back_send[0, low] = (back_part[1, low] + back_fwd[0].astype(f32)).astype(bf16)
    b_direct.append(send(back_send.at[0, low], back_recv.at[0, low], sem.back, (4,), at_y(1)))
    recv(b_high)
    back_send[2, high] = (back_part[3, high] + back_fwd[1].astype(f32)).astype(bf16)
    b_direct.append(send(back_send.at[2, high], back_recv.at[1, high], sem.back, (5,), at_y(3)))

    def y_gather(ref, cols, pair, lead):
        def place(d, rows=None):
            part = mod(y, d, 4)
            return ref.at[part, :, cols] if rows is None else ref.at[part, rows, cols]

        right = send(place(0), place(0), pair, lead + (0,), at_y(1))
        left = send(place(0), place(0), pair, lead + (1,), at_y(3))
        yield
        recv(right)
        on_right = send(place(3, low), place(3, low), pair, lead + (2,), at_y(1))
        recv(left)
        on_left = send(place(1, high), place(1, high), pair, lead + (3,), at_y(3))
        yield
        recv(on_right, on_left)
        yield

    for i in range(4):
        rows = span(mod(x, steps_x[i], 4), 64)
        own = pre_total(1, i)
        recv(across[i])
        h = own + r.half_recv[i].astype(f32)
        t = jnp.tanh(gelu_scale * (h + 0.044715 * h * h * h))
        act[y, rows, :] = (0.5 * h * (1.0 + t)).astype(bf16)
        r.slope[rows, :] = 0.5 * (1.0 + t) + 0.5 * h * (1.0 - t * t) * gelu_scale * (1.0 + 0.134145 * h * h)
    a_steps = y_gather(act, slice(None), sem.act, ())
    next(a_steps)
    recv(*b_direct)
    gph = []
    my_cols, other_cols = span(zh, 384), span(oh, 384)
    for i in range(4):
        rows = span(i, 64)
        total = back_part[0, rows] + back_recv[0, rows].astype(f32) + back_recv[1, rows].astype(f32)
        gp[y, rows, my_cols] = (total * r.slope[rows, :]).astype(bf16)
        place = gp.at[y, rows, my_cols]
        gph.append(send(place, place, sem.gph, (i,), at_z(4)))
    g_own = y_gather(gp, my_cols, sem.gp, (0,))
    next(g_own)

    def o_flow(d):
        q = mod(y, d, 4)
        part, own = r.o_part.at[d], r.o_own.at[d]
        part[...] = contract(act[q], w_out[...], 1, 0).reshape(4, 64, 1536)
        r.o_sib_send[d] = part[:, span(oc, 32), :].astype(bf16)
        swap = send(r.o_sib_send.at[d], r.o_sib_recv.at[d], sem.osib, (d,), sib)
        yield
        recv(swap)
        own[...] = part[:, span(c, 32), :] + r.o_sib_recv[d].astype(f32)

        def block(e):
            z_ = mod(z, e, 8)
            return own.at[:, span(z_ // 4, 16), span(lax.rem(z_, 4), 384)]

        halves = (pl.ds(0, 2), pl.ds(2, 2))
        ring = {}
        for step in range(4):
            for way in range(2):
                to_send, got = r.o_ring_send.at[d, way, step], r.o_ring_recv.at[d, way]
                e = 4 - step if way == 0 else 4 + step
                where = halves[way] if step == 0 else slice(None)
                if step:
                    recv(ring[way])
                if step == 0:
                    to_send[where] = block(e)[where].astype(bf16)
                elif step == 1:
                    with_, without = halves[way], halves[1 - way]
                    to_send[with_] = (block(e)[with_] + got[0, with_].astype(f32)).astype(bf16)
                    to_send[without] = block(e)[without].astype(bf16)
                else:
                    to_send[...] = (block(e)[...] + got[step - 1].astype(f32)).astype(bf16)
                ring[way] = send(
                    to_send.at[where], got.at[step, where], sem.oring, (d, way, step), at_z(1 if way == 0 else 7)
                )
            yield
        recv(ring[0], ring[1])
        got = r.o_ring_recv
        r.o_x_own[d] = block(0)[...] + got[d, 0, 3].astype(f32) + got[d, 1, 3].astype(f32)
        r.o_x_send[d] = r.o_x_own[d].astype(bf16)
        ox = [
            send(r.o_x_send.at[d, mod(x, e, 4)], r.o_x_recv.at[d, e - 1], sem.ox, (d, e - 1), at_x(e)) for e in (2, 1, 3)
        ]
        yield
        recv(*ox)
        total = r.o_x_own[d, x]
        for e in range(3):
            total = total + r.o_x_recv[d, e].astype(f32)
        r.o_fin[c, q] = total.astype(bf16)
        yield

    def g_flow(d):
        q = mod(y, d, 4)
        part, own = r.g_part.at[d], r.g_own.at[d]
        part[...] = contract(gp[q], w_mine[...], 1, 1).reshape(4, 64, 768)
        r.g_sib_send[d] = part[:, span(oc, 32), :].astype(bf16)
        swap = send(r.g_sib_send.at[d], r.g_sib_recv.at[d], sem.gsib, (d,), sib)
        yield
        recv(swap)
        own[...] = part[:, span(c, 32), :] + r.g_sib_recv[d].astype(f32)
        gx = []
        for e in (2, 1, 3):
            r.g_x_send[d, e - 1] = own[mod(x, e, 4)].astype(bf16)
            gx.append(send(r.g_x_send.at[d, e - 1], r.g_x_recv.at[d, e - 1], sem.gx, (d, e - 1), at_x(e)))
        yield
        recv(*gx)
        total = own[x]
        for e in range(3):
            total = total + r.g_x_recv[d, e].astype(f32)
        r.g_z_send[d] = total.astype(bf16)
        for s in range(2):
            for l in range(2):
                mine = jnp.logical_and(zh == s, zl == 2 * zh + l)
                piece = r.g_z_send.at[d, span(s, 16), span(l, 384)]
                send_unless(
                    mine, copy(piece, r.g_z_recv.at[d, zl], sem.gz, (d, s * 2 + l), dev(x, y, s * 4 + 2 * zh + l, c), (d, zl))
                )

                @pl.when(mine)
                def _():
                    r.g_z_recv[d, zl] = piece[...]

        yield
        for j in range(4):
            recv_unless(
                jnp.logical_and(half == zh, zl == j),
                copy(r.g_z_send.at[d, span(0, 16), span(0, 384)], r.g_z_recv.at[d, j], sem.gz, (d, 0), sib, (d, j)),
            )
        total = r.g_z_recv[d, 0].astype(f32)
        for j in range(1, 4):
            total = total + r.g_z_recv[d, j].astype(f32)
        r.g_fin[c, q] = total.astype(bf16)
        yield

    gi, gi_own = [], []

    def gi_flow():
        for b, which in enumerate((zh, oh)):
            for p in range(2):
                rows = span(p, 384)
                r.gi_send[rows, span(b, 384)] = contract(
                    tok_all[:, :, :, rows].reshape(1024, 384), gp[:, :, span(which, 384)].reshape(1024, 384), 0, 0
                ).astype(bf16)
            for d in (2, 1, 3):
                gi.append(
                    send(
                        r.gi_send.at[span(mod(x, d, 4), 192), span(b, 384)], grad_in.at[:, w_cols(which, x)],
                        sem.gi, (b, d - 1), at_x(d),
                    )
                )
            gi_own.append(load(r.gi_send.at[span(x, 192), span(b, 384)], grad_in.at[:, w_cols(which, x)]))
            yield

    def go_flow():
        for n in range(4):
            cols = span(n, 384)
            grad_out[:, cols] = contract(
                act[...].reshape(1024, 384), cot_all[:, :, :, cols].reshape(1024, 384), 0, 0
            ).astype(bf16)
            yield

    def other_flow():
        recv(*gph)
        yield from y_gather(gp, other_cols, sem.gp, (1,))

    o = {d: o_flow(d) for d in range(4)}
    g = {d: g_flow(d) for d in range(4)}
    o0, o1, o2, o3 = o[0], o[1], o[2], o[3]
    g0, g1, g2, g3 = g[0], g[1], g[2], g[3]
    a, mine, other, gi_steps, go = a_steps, g_own, other_flow(), gi_flow(), go_flow()
    for flow in (o0, o0, a, o1, o1, mine, o3, o3, o0, other, g0, a, o2, g0, o2, o0, o1, mine, gi_steps, o3, other, g1, g3, g1, g3, o0, o1, o2, other, g2, g2, gi_steps, g0, o0, o1, o3, g1, g3, o2, o3, go, g2, o1, o2, go, o3, o0, g0, g1, g3, o2, go):
        next(flow)
    for flow in (g0, g1, g3, g2):
        for _ in flow:
            pass
    g_last = send(r.g_fin.at[c], r.g_fin.at[c], sem.gfin, (0,), sib)
    for flow in (o0, o1, o3, o2):
        for _ in flow:
            pass
    o_last = send(r.o_fin.at[c], r.o_fin.at[c], sem.ofin, (0,), sib)
    for _ in go:
        pass
    stored = load(grad_out, grad_out_hbm)

    row = lax.broadcasted_iota(jnp.int32, (384, 192), 0)
    col = lax.broadcasted_iota(jnp.int32, (384, 192), 1)
    take = jnp.where(row == col + 192 * c, 1.0, 0.0).astype(bf16)
    recv(o_last)
    out[...] = contract(take, r.o_fin[...].reshape(128, 384), 0, 1).astype(bf16)
    recv(g_last)
    grad_tok[...] = contract(take, r.g_fin[...].reshape(128, 384), 0, 1).astype(bf16)
    recv(*gi)
    stored.wait()
    for one in gi_own:
        one.wait()
    assert not coming
    for one in started:
        one.wait_send()
    for mine, one in maybe:

        @pl.when(jnp.logical_not(mine))
        def _():
            one.wait_send()


def hand_over(*refs):
    loads = [pltpu.make_async_copy(refs[i], refs[8 + i], refs[12].at[i]) for i in range(4)]
    stores = [pltpu.make_async_copy(refs[8 + i], refs[4 + i], refs[12].at[4 + i]) for i in range(4)]
    for one in loads:
        one.start()
    for one, then in zip(loads, stores):
        one.wait()
        then.start()
    for one in stores:
        one.wait()


def on_device(tokens, w_in, w_out, cotangent):
    scratch = [pltpu.VMEM(dims, dtype) for dims, dtype in buffers().values()]
    for dims in semaphores().values():
        scratch += [pltpu.SemaphoreType.DMA(dims)] * 2
    scratch.append(pltpu.SemaphoreType.DMA((8,)))
    shape = jax.ShapeDtypeStruct
    vmem, hbm = pl.BlockSpec(memory_space=pltpu.VMEM), pl.BlockSpec(memory_space=pl.ANY)
    shapes = (shape((192, 128), bf16), shape((192, 128), bf16), shape((192, 3072), bf16), shape((384, 1536), bf16))
    results = pl.pallas_call(
        kernel,
        out_shape=shapes,
        in_specs=[hbm] * 4,
        out_specs=[vmem, vmem, hbm, hbm],
        scratch_shapes=scratch,
        compiler_params=pltpu.CompilerParams(
            collective_id=0, has_side_effects=True, vmem_limit_bytes=60 * 1024 * 1024
        ),
        cost_estimate=pl.CostEstimate(flops=7_250_000_000, bytes_accessed=5_000_000, transcendentals=100_000),
    )(tokens.T, w_in, w_out, cotangent.T)
    out, grad_tokens, grad_in, grad_out = pl.pallas_call(
        hand_over,
        out_shape=shapes,
        in_specs=[hbm] * 4,
        out_specs=[hbm] * 4,
        scratch_shapes=[pltpu.VMEM(one.shape, one.dtype) for one in shapes] + [pltpu.SemaphoreType.DMA((8,))],
    )(*results)
    return out.T, grad_tokens.T, grad_in, grad_out


def solution(mesh):
    specs = (P("gx", ("gz", "gy")), P(("gz", "gx"), "gy"), P(("gy", "gx"), "gz"))
    return jax.shard_map(
        on_device,
        mesh=mesh,
        in_specs=(specs[0], specs[1], specs[2], specs[0]),
        out_specs=(specs[0], specs[0], specs[1], specs[2]),
        check_vma=False,
    )
```

```python
import types

import jax
import jax.numpy as jnp
from jax import lax
from jax.experimental import pallas as pl
from jax.experimental.pallas import tpu as pltpu
from jax.sharding import PartitionSpec as P

MESH = pl.DeviceIdType.MESH
gelu_scale = 0.7978845608
bf16, f32 = jnp.bfloat16, jnp.float32


def contract(left, right, left_dim, right_dim):
    return lax.dot_general(
        left, right, (((left_dim,), (right_dim,)), ((), ())), preferred_element_type=f32
    )


def buffers():
    return dict(
        tok=((192, 128), bf16), cot=((192, 128), bf16), w_out=((384, 1536), bf16), grad_out=((384, 1536), bf16),
        tok_sib=((192, 128), bf16), cot_sib=((192, 128), bf16),
        tok_chip=((2, 4, 16, 384), bf16), cot_chip=((2, 4, 16, 384), bf16),
        tok_all=((4, 4, 64, 768), bf16), cot_all=((4, 4, 64, 1536), bf16), w_mine=((768, 768), bf16),
        pre_part=((2, 4, 4, 64, 384), f32), pre_send=((2, 4, 3, 64, 384), bf16),
        pre_fwd=((2, 4, 64, 384), bf16), pre_recv=((2, 4, 2, 64, 384), bf16),
        half_send=((4, 64, 384), bf16), half_recv=((4, 64, 384), bf16),
        back_part=((4, 256, 384), f32), back_send=((3, 256, 384), bf16),
        back_fwd=((2, 128, 384), bf16), back_recv=((2, 256, 384), bf16), slope=((256, 384), f32),
        act=((4, 256, 384), bf16), gp=((4, 256, 768), bf16),
        o_part=((4, 4, 64, 1536), f32), o_sib_send=((4, 4, 32, 1536), bf16), o_sib_recv=((4, 4, 32, 1536), bf16),
        o_own=((4, 4, 32, 1536), f32), o_ring_send=((4, 2, 4, 4, 16, 384), bf16), o_ring_recv=((4, 2, 4, 4, 16, 384), bf16),
        o_x_send=((4, 4, 16, 384), bf16), o_x_recv=((4, 3, 16, 384), bf16), o_x_own=((4, 4, 16, 384), f32),
        o_fin=((2, 4, 16, 384), bf16),
        g_part=((4, 4, 64, 768), f32), g_sib_send=((4, 4, 32, 768), bf16), g_sib_recv=((4, 4, 32, 768), bf16),
        g_own=((4, 4, 32, 768), f32), g_x_send=((4, 3, 32, 768), bf16), g_x_recv=((4, 3, 32, 768), bf16),
        g_z_send=((4, 32, 768), bf16), g_z_recv=((4, 4, 16, 384), bf16),
        g_fin=((2, 4, 16, 384), bf16), gi_send=((768, 768), bf16),
    )


def semaphores():
    return dict(
        inp=(2,), w=(3, 2), tz=(4,), cx=(3,), cz=(2, 4, 2), csib=(8, 2), tx=(3,), tsib=(4,),
        pre=(2, 4, 3), half=(4,), back=(6,), act=(4,), gp=(2, 4), gph=(4,),
        osib=(4,), oring=(4, 2, 4), ox=(4, 3), ofin=(1,),
        gsib=(4,), gx=(4, 3), gz=(4, 4), gfin=(1,), gi=(2, 3),
    )


def kernel(*refs):
    tok_hbm, w_in, w_out_hbm, cot_hbm, out, grad_tok, grad_in, grad_out_hbm = refs[:8]
    bufs = buffers()
    r = types.SimpleNamespace(**dict(zip(bufs, refs[8:])))
    rest = refs[8 + len(bufs):]
    local = rest[-1]
    sem = types.SimpleNamespace(**{name: rest[2 * i : 2 * i + 2] for i, name in enumerate(semaphores())})
    tok_all, cot_all, w_mine, act, gp = r.tok_all, r.cot_all, r.w_mine, r.act, r.gp

    ax, ay, y = lax.axis_index("gx"), lax.axis_index("gy"), lax.axis_index("gz")
    zh, x = ax // 4, lax.rem(ax, 4)
    zl, c = ay // 2, lax.rem(ay, 2)
    z = zh * 4 + zl
    oc, oh = 1 - c, 1 - zh

    def dev(x_, y_, z_, c_):
        return (z_ // 4 * 4 + x_, lax.rem(z_, 4) * 2 + c_, y_)

    def mod(v, d, n):
        return lax.rem(v + d, n)

    def at_x(d):
        return dev(mod(x, d, 4), y, z, c)

    def at_y(d):
        return dev(x, mod(y, d, 4), z, c)

    def at_z(d):
        return dev(x, y, mod(z, d, 8), c)

    sib = dev(x, y, z, oc)
    started, coming, maybe = [], [], []

    def copy(src, dst, pair, index, to, from_index=None):
        ss, rs = pair
        return pltpu.make_async_remote_copy(
            src_ref=src, dst_ref=dst, send_sem=ss.at[index], recv_sem=rs.at[index if from_index is None else from_index],
            device_id=to, device_id_type=MESH,
        )

    def send(src, dst, pair, index, to):
        one = copy(src, dst, pair, index, to)
        one.start()
        started.append(one)
        coming.append(one)
        return one

    def recv(*copies):
        for one in copies:
            one.wait_recv()
            coming[:] = [other for other in coming if other is not one]

    def send_unless(mine, one):
        maybe.append((mine, one))

        @pl.when(jnp.logical_not(mine))
        def _():
            one.start()

    def recv_unless(mine, one):
        @pl.when(jnp.logical_not(mine))
        def _():
            one.wait_recv()

    def span(i, n):
        return pl.ds(i * n if isinstance(i, int) else pl.multiple_of(i * n, n), n)

    tok, cot, w_out, grad_out = r.tok, r.cot, r.w_out, r.grad_out
    loads = []

    def load(src, dst):
        one = pltpu.make_async_copy(src, dst, local.at[len(loads)])
        one.start()
        loads.append(one)
        return one

    t_load, c_load = load(tok_hbm, tok), load(cot_hbm, cot)

    barrier = pltpu.get_barrier_semaphore()
    peers = [at_x(d) for d in (1, 2, 3)] + [at_y(d) for d in (1, 2, 3)] + [at_z(d) for d in range(1, 8)] + [sib]
    for peer in peers:
        pl.semaphore_signal(barrier, inc=1, device_id=peer, device_id_type=MESH)
    pl.semaphore_wait(barrier, len(peers))

    t_load.wait()
    c_load.wait()
    t_in = send(tok, r.tok_sib, sem.inp, 0, sib)
    c_in = send(cot, r.cot_sib, sem.inp, 1, sib)

    def w_cols(block, x_):
        return span(block * 4 + x_, 384)

    w_copies = [
        send(w_in.at[:, w_cols(b, mod(x, d, 4))], w_mine.at[span(x, 192), span(b, 384)], sem.w, (d - 1, b), at_x(d))
        for d in (2,)
        for b in range(2)
    ]

    w_loads = [load(w_in.at[:, w_cols(b, x)], w_mine.at[span(x, 192), span(b, 384)]) for b in range(2)]
    w_out_load = load(w_out_hbm, w_out)

    row = lax.broadcasted_iota(jnp.int32, (192, 384), 0)
    col = lax.broadcasted_iota(jnp.int32, (192, 384), 1)
    put_own = jnp.where(col == row + 192 * c, 1.0, 0.0).astype(bf16)
    put_sib = jnp.where(col == row + 192 * oc, 1.0, 0.0).astype(bf16)

    def chip(own, other):
        both = contract(own[...], put_own, 0, 0) + contract(other[...], put_sib, 0, 0)
        return both.astype(bf16).reshape(2, 4, 16, 384)

    recv(t_in)
    r.tok_chip[...] = chip(tok, r.tok_sib)

    half, l_mine = zl // 2, lax.rem(zl, 2)
    my16 = span(c * 2 + zh, 16)
    t_piece, t_place = r.tok_chip.at[c], tok_all.at[:, x, my16, span(l_mine, 384)]
    for j in (0, 1, 2, 3):
        send_unless(
            jnp.logical_and(half == zh, zl == j),
            copy(t_piece, t_place, sem.tz, (j,), dev(x, y, half * 4 + j, c), (zh * 2 + l_mine,)),
        )

    @pl.when(half == zh)
    def _():
        t_place[...] = t_piece[...]

    recv(c_in)
    r.cot_chip[...] = chip(cot, r.cot_sib)
    c_piece, c_place = r.cot_chip.at[c], cot_all.at[:, x, my16, span(zl, 384)]
    cx = [send(c_piece, c_place, sem.cx, (d - 1,), at_x(d)) for d in (2, 1, 3)]
    c_place[...] = c_piece[...]
    w_copies += [
        send(w_in.at[:, w_cols(b, mod(x, d, 4))], w_mine.at[span(x, 192), span(b, 384)], sem.w, (d - 1, b), at_x(d))
        for d in (1, 3)
        for b in range(2)
    ]


    def c_flow():
        c_sib = []

        def block(d, k):
            z_ = mod(z, d + 8, 8)
            return cot_all.at[span(k, 2), :, span(c * 2 + z_ // 4, 16), span(lax.rem(z_, 4), 384)]

        def onward(d, k, way, s):
            return send(block(d, k), block(d, k), sem.cz, (way, s, k), at_z(1 if way == 0 else 7))

        def to_sib(d, k):
            c_sib.append(send(block(d, k), block(d, k), sem.csib, (d % 8, k), sib))

        recv(*cx)
        ring = {}
        for k in range(2):
            for way in range(2):
                ring[way, k] = onward(0, k, way, 0)
        for k in range(2):
            to_sib(0, k)
        yield
        for s in range(1, 4):
            for k in range(2):
                for way in range(2):
                    recv(ring[way, k])
                    d = -s if way == 0 else s
                    if s < 3 or k == way:
                        ring[way, k] = onward(d, k, way, s)
                    to_sib(d, k)
            yield
        for k in range(2):
            recv(ring[k, k])
            to_sib(4, k)
        yield
        recv(*c_sib)
        yield

    c_steps = c_flow()
    next(c_steps)

    for s in range(2):
        for l in range(2):
            recv_unless(
                jnp.logical_and(zh == s, zl == 2 * zh + l), copy(t_piece, t_place, sem.tz, (0,), sib, (s * 2 + l,))
            )

    def t_rows(d):
        return tok_all.at[:, mod(x, d, 4), span(c, 32)]

    tx = {d: send(t_rows(0), t_rows(0), sem.tx, (d - 1,), at_x(d)) for d in (1, 3, 2)}
    t_sib = {0: send(t_rows(0), t_rows(0), sem.tsib, (0,), sib)}

    def t_arrive(d):
        recv(tx[4 - d])
        t_sib[d] = send(t_rows(d), t_rows(d), sem.tsib, (d,), sib)

    steps_x = (0, 1, 3, 2)
    blocks = (oh, zh)
    fwd, direct, joined = {}, {}, {}

    def pre_block(i):
        d = steps_x[i]
        recv(t_sib[d])
        rows = tok_all[:, mod(x, d, 4)].reshape(256, 768)
        near, far = (1, 3) if i % 2 == 0 else (3, 1)
        for b in range(2):
            r.pre_part[b, i] = contract(rows, w_mine[:, span(blocks[b], 384)], 1, 0).reshape(4, 64, 384)
            for j, to in ((0, near), (1, far)):
                whose = 2 if j == 0 else far
                r.pre_send[b, i, j] = r.pre_part[b, i, mod(y, whose, 4)].astype(bf16)
                src = r.pre_send.at[b, i, j]
                if j == 0:
                    fwd[b, i] = send(src, r.pre_fwd.at[b, i], sem.pre, (b, i, 0), at_y(to))
                else:
                    direct[b, i] = send(src, r.pre_recv.at[b, i, 0], sem.pre, (b, i, 1), at_y(to))

    def pre_join(b, i):
        near = 1 if i % 2 == 0 else 3
        recv(fwd[b, i])
        r.pre_send[b, i, 2] = (r.pre_part[b, i, mod(y, near, 4)] + r.pre_fwd[b, i].astype(f32)).astype(bf16)
        joined[b, i] = send(r.pre_send.at[b, i, 2], r.pre_recv.at[b, i, 1], sem.pre, (b, i, 2), at_y(near))

    def pre_total(b, i):
        recv(direct[b, i], joined[b, i])
        return r.pre_part[b, i, y] + r.pre_recv[b, i, 0].astype(f32) + r.pre_recv[b, i, 1].astype(f32)

    across = {}

    def pre_across(i):
        r.half_send[i] = pre_total(0, i).astype(bf16)
        across[i] = send(r.half_send.at[i], r.half_recv.at[i], sem.half, (i,), at_z(4))

    next(c_steps)
    for one in w_loads:
        one.wait()
    recv(*w_copies)
    pre_block(0)
    next(c_steps)
    t_arrive(1)
    t_arrive(3)
    pre_block(1)
    pre_join(0, 0)
    pre_join(1, 0)
    pre_block(2)
    next(c_steps)
    t_arrive(2)
    pre_join(0, 1)
    pre_join(1, 1)
    pre_block(3)
    pre_across(0)
    pre_join(0, 2)
    pre_join(1, 2)
    pre_across(1)
    next(c_steps)
    pre_join(0, 3)
    pre_join(1, 3)
    pre_across(2)
    next(c_steps)

    low, high = span(0, 128), span(1, 128)
    back_part, back_send, back_recv, back_fwd = r.back_part, r.back_send, r.back_recv, r.back_fwd
    w_out_load.wait()
    for d in (2, 1, 3, 0):
        back_part[d] = contract(cot_all[mod(y, d, 4)].reshape(256, 1536), w_out[...], 1, 1)
        if d == 2:
            back_send[1] = back_part[2].astype(bf16)
            b_low = send(back_send.at[1, low], back_fwd.at[0], sem.back, (0,), at_y(1))
            b_high = send(back_send.at[1, high], back_fwd.at[1], sem.back, (1,), at_y(3))
        elif d == 1:
            back_send[0, high] = back_part[1, high].astype(bf16)
            b_direct = [send(back_send.at[0, high], back_recv.at[0, high], sem.back, (2,), at_y(1))]
        elif d == 3:
            back_send[2, low] = back_part[3, low].astype(bf16)
            b_direct.append(send(back_send.at[2, low], back_recv.at[1, low], sem.back, (3,), at_y(3)))
    pre_across(3)
    recv(b_low)
    back_send[0, low] = (back_part[1, low] + back_fwd[0].astype(f32)).astype(bf16)
    b_direct.append(send(back_send.at[0, low], back_recv.at[0, low], sem.back, (4,), at_y(1)))
    recv(b_high)
    back_send[2, high] = (back_part[3, high] + back_fwd[1].astype(f32)).astype(bf16)
    b_direct.append(send(back_send.at[2, high], back_recv.at[1, high], sem.back, (5,), at_y(3)))

    def y_gather(ref, cols, pair, lead):
        def place(d, rows=None):
            part = mod(y, d, 4)
            return ref.at[part, :, cols] if rows is None else ref.at[part, rows, cols]

        right = send(place(0), place(0), pair, lead + (0,), at_y(1))
        left = send(place(0), place(0), pair, lead + (1,), at_y(3))
        yield
        recv(right)
        on_right = send(place(3, low), place(3, low), pair, lead + (2,), at_y(1))
        recv(left)
        on_left = send(place(1, high), place(1, high), pair, lead + (3,), at_y(3))
        yield
        recv(on_right, on_left)
        yield

    for i in range(4):
        rows = span(mod(x, steps_x[i], 4), 64)
        own = pre_total(1, i)
        recv(across[i])
        h = own + r.half_recv[i].astype(f32)
        t = jnp.tanh(gelu_scale * (h + 0.044715 * h * h * h))
        act[y, rows, :] = (0.5 * h * (1.0 + t)).astype(bf16)
        r.slope[rows, :] = 0.5 * (1.0 + t) + 0.5 * h * (1.0 - t * t) * gelu_scale * (1.0 + 0.134145 * h * h)
    a_steps = y_gather(act, slice(None), sem.act, ())
    next(a_steps)
    recv(*b_direct)
    gph = []
    my_cols, other_cols = span(zh, 384), span(oh, 384)
    for i in range(4):
        rows = span(i, 64)
        total = back_part[0, rows] + back_recv[0, rows].astype(f32) + back_recv[1, rows].astype(f32)
        gp[y, rows, my_cols] = (total * r.slope[rows, :]).astype(bf16)
        place = gp.at[y, rows, my_cols]
        gph.append(send(place, place, sem.gph, (i,), at_z(4)))
    g_own = y_gather(gp, my_cols, sem.gp, (0,))
    next(g_own)

    def o_flow(d):
        q = mod(y, d, 4)
        part, own = r.o_part.at[d], r.o_own.at[d]
        part[...] = contract(act[q], w_out[...], 1, 0).reshape(4, 64, 1536)
        r.o_sib_send[d] = part[:, span(oc, 32), :].astype(bf16)
        swap = send(r.o_sib_send.at[d], r.o_sib_recv.at[d], sem.osib, (d,), sib)
        yield
        recv(swap)
        own[...] = part[:, span(c, 32), :] + r.o_sib_recv[d].astype(f32)

        def block(e):
            z_ = mod(z, e, 8)
            return own.at[:, span(z_ // 4, 16), span(lax.rem(z_, 4), 384)]

        halves = (pl.ds(0, 2), pl.ds(2, 2))
        ring = {}
        for step in range(4):
            for way in range(2):
                to_send, got = r.o_ring_send.at[d, way, step], r.o_ring_recv.at[d, way]
                e = 4 - step if way == 0 else 4 + step
                where = halves[way] if step == 0 else slice(None)
                if step:
                    recv(ring[way])
                if step == 0:
                    to_send[where] = block(e)[where].astype(bf16)
                elif step == 1:
                    with_, without = halves[way], halves[1 - way]
                    to_send[with_] = (block(e)[with_] + got[0, with_].astype(f32)).astype(bf16)
                    to_send[without] = block(e)[without].astype(bf16)
                else:
                    to_send[...] = (block(e)[...] + got[step - 1].astype(f32)).astype(bf16)
                ring[way] = send(
                    to_send.at[where], got.at[step, where], sem.oring, (d, way, step), at_z(1 if way == 0 else 7)
                )
            yield
        recv(ring[0], ring[1])
        got = r.o_ring_recv
        r.o_x_own[d] = block(0)[...] + got[d, 0, 3].astype(f32) + got[d, 1, 3].astype(f32)
        r.o_x_send[d] = r.o_x_own[d].astype(bf16)
        ox = [
            send(r.o_x_send.at[d, mod(x, e, 4)], r.o_x_recv.at[d, e - 1], sem.ox, (d, e - 1), at_x(e)) for e in (2, 1, 3)
        ]
        yield
        recv(*ox)
        total = r.o_x_own[d, x]
        for e in range(3):
            total = total + r.o_x_recv[d, e].astype(f32)
        r.o_fin[c, q] = total.astype(bf16)
        yield

    def g_flow(d):
        q = mod(y, d, 4)
        part, own = r.g_part.at[d], r.g_own.at[d]
        part[...] = contract(gp[q], w_mine[...], 1, 1).reshape(4, 64, 768)
        r.g_sib_send[d] = part[:, span(oc, 32), :].astype(bf16)
        swap = send(r.g_sib_send.at[d], r.g_sib_recv.at[d], sem.gsib, (d,), sib)
        yield
        recv(swap)
        own[...] = part[:, span(c, 32), :] + r.g_sib_recv[d].astype(f32)
        gx = []
        for e in (2, 1, 3):
            r.g_x_send[d, e - 1] = own[mod(x, e, 4)].astype(bf16)
            gx.append(send(r.g_x_send.at[d, e - 1], r.g_x_recv.at[d, e - 1], sem.gx, (d, e - 1), at_x(e)))
        yield
        recv(*gx)
        total = own[x]
        for e in range(3):
            total = total + r.g_x_recv[d, e].astype(f32)
        r.g_z_send[d] = total.astype(bf16)
        for s in range(2):
            for l in range(2):
                mine = jnp.logical_and(zh == s, zl == 2 * zh + l)
                piece = r.g_z_send.at[d, span(s, 16), span(l, 384)]
                send_unless(
                    mine, copy(piece, r.g_z_recv.at[d, zl], sem.gz, (d, s * 2 + l), dev(x, y, s * 4 + 2 * zh + l, c), (d, zl))
                )

                @pl.when(mine)
                def _():
                    r.g_z_recv[d, zl] = piece[...]

        yield
        for j in range(4):
            recv_unless(
                jnp.logical_and(half == zh, zl == j),
                copy(r.g_z_send.at[d, span(0, 16), span(0, 384)], r.g_z_recv.at[d, j], sem.gz, (d, 0), sib, (d, j)),
            )
        total = r.g_z_recv[d, 0].astype(f32)
        for j in range(1, 4):
            total = total + r.g_z_recv[d, j].astype(f32)
        r.g_fin[c, q] = total.astype(bf16)
        yield

    gi, gi_own = [], []

    def gi_flow():
        for b, which in enumerate((zh, oh)):
            for p in range(2):
                rows = span(p, 384)
                r.gi_send[rows, span(b, 384)] = contract(
                    tok_all[:, :, :, rows].reshape(1024, 384), gp[:, :, span(which, 384)].reshape(1024, 384), 0, 0
                ).astype(bf16)
            for d in (2, 1, 3):
                gi.append(
                    send(
                        r.gi_send.at[span(mod(x, d, 4), 192), span(b, 384)], grad_in.at[:, w_cols(which, x)],
                        sem.gi, (b, d - 1), at_x(d),
                    )
                )
            gi_own.append(load(r.gi_send.at[span(x, 192), span(b, 384)], grad_in.at[:, w_cols(which, x)]))
            yield

    def go_flow():
        for n in range(4):
            cols = span(n, 384)
            grad_out[:, cols] = contract(
                act[...].reshape(1024, 384), cot_all[:, :, :, cols].reshape(1024, 384), 0, 0
            ).astype(bf16)
            yield

    def other_flow():
        recv(*gph)
        yield from y_gather(gp, other_cols, sem.gp, (1,))

    o = {d: o_flow(d) for d in range(4)}
    g = {d: g_flow(d) for d in range(4)}
    o0, o1, o2, o3 = o[0], o[1], o[2], o[3]
    g0, g1, g2, g3 = g[0], g[1], g[2], g[3]
    a, mine, other, gi_steps, go = a_steps, g_own, other_flow(), gi_flow(), go_flow()
    for flow in (o0, o0, a, o1, o1, mine, o3, o3, o0, other, g0, a, o2, g0, o2, o0, o1, mine, gi_steps, o3, other, g1, g3, g1, g3, o0, o1, o2, other, g2, g2, gi_steps, g0, o0, o1, o3, g1, g3, o2, o3, go, g2, o1, o2, go, o3, o0, g0, g1, g3, o2, go):
        next(flow)
    for flow in (g0, g1, g3, g2):
        for _ in flow:
            pass
    g_last = send(r.g_fin.at[c], r.g_fin.at[c], sem.gfin, (0,), sib)
    for flow in (o0, o1, o3, o2):
        for _ in flow:
            pass
    o_last = send(r.o_fin.at[c], r.o_fin.at[c], sem.ofin, (0,), sib)
    for _ in go:
        pass
    stored = load(grad_out, grad_out_hbm)

    row = lax.broadcasted_iota(jnp.int32, (384, 192), 0)
    col = lax.broadcasted_iota(jnp.int32, (384, 192), 1)
    take = jnp.where(row == col + 192 * c, 1.0, 0.0).astype(bf16)
    recv(o_last)
    out[...] = contract(take, r.o_fin[...].reshape(128, 384), 0, 1).astype(bf16)
    recv(g_last)
    grad_tok[...] = contract(take, r.g_fin[...].reshape(128, 384), 0, 1).astype(bf16)
    recv(*gi)
    stored.wait()
    for one in gi_own:
        one.wait()
    assert not coming
    for one in started:
        one.wait_send()
    for mine, one in maybe:

        @pl.when(jnp.logical_not(mine))
        def _():
            one.wait_send()


def hand_over(*refs):
    loads = [pltpu.make_async_copy(refs[i], refs[8 + i], refs[12].at[i]) for i in range(4)]
    stores = [pltpu.make_async_copy(refs[8 + i], refs[4 + i], refs[12].at[4 + i]) for i in range(4)]
    for one in loads:
        one.start()
    for one, then in zip(loads, stores):
        one.wait()
        then.start()
    for one in stores:
        one.wait()


def on_device(tokens, w_in, w_out, cotangent):
    scratch = [pltpu.VMEM(dims, dtype) for dims, dtype in buffers().values()]
    for dims in semaphores().values():
        scratch += [pltpu.SemaphoreType.DMA(dims)] * 2
    scratch.append(pltpu.SemaphoreType.DMA((8,)))
    shape = jax.ShapeDtypeStruct
    vmem, hbm = pl.BlockSpec(memory_space=pltpu.VMEM), pl.BlockSpec(memory_space=pl.ANY)
    shapes = (shape((192, 128), bf16), shape((192, 128), bf16), shape((192, 3072), bf16), shape((384, 1536), bf16))
    results = pl.pallas_call(
        kernel,
        out_shape=shapes,
        in_specs=[hbm] * 4,
        out_specs=[vmem, vmem, hbm, hbm],
        scratch_shapes=scratch,
        compiler_params=pltpu.CompilerParams(
            collective_id=0, has_side_effects=True, vmem_limit_bytes=60 * 1024 * 1024
        ),
        cost_estimate=pl.CostEstimate(flops=7_250_000_000, bytes_accessed=5_000_000, transcendentals=100_000),
    )(tokens.T, w_in, w_out, cotangent.T)
    out, grad_tokens, grad_in, grad_out = pl.pallas_call(
        hand_over,
        out_shape=shapes,
        in_specs=[hbm] * 4,
        out_specs=[hbm] * 4,
        scratch_shapes=[pltpu.VMEM(one.shape, one.dtype) for one in shapes] + [pltpu.SemaphoreType.DMA((8,))],
    )(*results)
    return out.T, grad_tokens.T, grad_in, grad_out


def solution(mesh):
    specs = (P("gx", ("gz", "gy")), P(("gz", "gx"), "gy"), P(("gy", "gx"), "gz"))
    return jax.shard_map(
        on_device,
        mesh=mesh,
        in_specs=(specs[0], specs[1], specs[2], specs[0]),
        out_specs=(specs[0], specs[0], specs[1], specs[2]),
        check_vma=False,
    )
```

```python
import types

import jax
import jax.numpy as jnp
from jax import lax
from jax.experimental import pallas as pl
from jax.experimental.pallas import tpu as pltpu
from jax.sharding import PartitionSpec as P

MESH = pl.DeviceIdType.MESH
gelu_scale = 0.7978845608
bf16, f32 = jnp.bfloat16, jnp.float32


def contract(left, right, left_dim, right_dim):
    return lax.dot_general(
        left, right, (((left_dim,), (right_dim,)), ((), ())), preferred_element_type=f32
    )


def buffers():
    return dict(
        tok=((192, 128), bf16), cot=((192, 128), bf16), w_out=((384, 1536), bf16), grad_out=((384, 1536), bf16),
        tok_sib=((192, 128), bf16), cot_sib=((192, 128), bf16),
        tok_chip=((2, 4, 16, 384), bf16), cot_chip=((2, 4, 16, 384), bf16),
        tok_all=((4, 4, 64, 768), bf16), cot_all=((4, 4, 64, 1536), bf16), w_mine=((768, 768), bf16),
        pre_part=((2, 4, 4, 64, 384), f32), pre_send=((2, 4, 3, 64, 384), bf16),
        pre_fwd=((2, 4, 64, 384), bf16), pre_recv=((2, 4, 2, 64, 384), bf16),
        half_send=((4, 64, 384), bf16), half_recv=((4, 64, 384), bf16),
        back_part=((4, 256, 384), f32), back_send=((3, 256, 384), bf16),
        back_fwd=((2, 128, 384), bf16), back_recv=((2, 256, 384), bf16), slope=((256, 384), f32),
        act=((4, 256, 384), bf16), gp=((4, 256, 768), bf16),
        o_part=((4, 4, 64, 1536), f32), o_sib_send=((4, 4, 32, 1536), bf16), o_sib_recv=((4, 4, 32, 1536), bf16),
        o_own=((4, 4, 32, 1536), f32), o_ring_send=((4, 2, 4, 4, 16, 384), bf16), o_ring_recv=((4, 2, 4, 4, 16, 384), bf16),
        o_x_send=((4, 4, 16, 384), bf16), o_x_recv=((4, 3, 16, 384), bf16), o_x_own=((4, 4, 16, 384), f32),
        o_fin=((2, 4, 16, 384), bf16),
        g_part=((4, 4, 64, 768), f32), g_sib_send=((4, 4, 32, 768), bf16), g_sib_recv=((4, 4, 32, 768), bf16),
        g_own=((4, 4, 32, 768), f32), g_x_send=((4, 3, 32, 768), bf16), g_x_recv=((4, 3, 32, 768), bf16),
        g_z_send=((4, 32, 768), bf16), g_z_recv=((4, 4, 16, 384), bf16),
        g_fin=((2, 4, 16, 384), bf16), gi_send=((768, 768), bf16),
    )


def semaphores():
    return dict(
        inp=(2,), w=(3, 2), tz=(4,), cx=(3,), cz=(2, 4, 2), csib=(8, 2), tx=(3,), tsib=(4,),
        pre=(2, 4, 3), half=(4,), back=(6,), act=(4,), gp=(2, 4), gph=(4,),
        osib=(4,), oring=(4, 2, 4), ox=(4, 3), ofin=(1,),
        gsib=(4,), gx=(4, 3), gz=(4, 4), gfin=(1,), gi=(2, 3),
    )


def kernel(*refs):
    tok_hbm, w_in, w_out_hbm, cot_hbm, out, grad_tok, grad_in, grad_out_hbm = refs[:8]
    bufs = buffers()
    r = types.SimpleNamespace(**dict(zip(bufs, refs[8:])))
    rest = refs[8 + len(bufs):]
    local = rest[-1]
    sem = types.SimpleNamespace(**{name: rest[2 * i : 2 * i + 2] for i, name in enumerate(semaphores())})
    tok_all, cot_all, w_mine, act, gp = r.tok_all, r.cot_all, r.w_mine, r.act, r.gp

    ax, ay, y = lax.axis_index("gx"), lax.axis_index("gy"), lax.axis_index("gz")
    zh, x = ax // 4, lax.rem(ax, 4)
    zl, c = ay // 2, lax.rem(ay, 2)
    z = zh * 4 + zl
    oc, oh = 1 - c, 1 - zh

    def dev(x_, y_, z_, c_):
        return (z_ // 4 * 4 + x_, lax.rem(z_, 4) * 2 + c_, y_)

    def mod(v, d, n):
        return lax.rem(v + d, n)

    def at_x(d):
        return dev(mod(x, d, 4), y, z, c)

    def at_y(d):
        return dev(x, mod(y, d, 4), z, c)

    def at_z(d):
        return dev(x, y, mod(z, d, 8), c)

    sib = dev(x, y, z, oc)
    started, coming, maybe = [], [], []

    def copy(src, dst, pair, index, to, from_index=None):
        ss, rs = pair
        return pltpu.make_async_remote_copy(
            src_ref=src, dst_ref=dst, send_sem=ss.at[index], recv_sem=rs.at[index if from_index is None else from_index],
            device_id=to, device_id_type=MESH,
        )

    def send(src, dst, pair, index, to):
        one = copy(src, dst, pair, index, to)
        one.start()
        started.append(one)
        coming.append(one)
        return one

    def recv(*copies):
        for one in copies:
            one.wait_recv()
            coming[:] = [other for other in coming if other is not one]

    def send_unless(mine, one):
        maybe.append((mine, one))

        @pl.when(jnp.logical_not(mine))
        def _():
            one.start()

    def recv_unless(mine, one):
        @pl.when(jnp.logical_not(mine))
        def _():
            one.wait_recv()

    def span(i, n):
        return pl.ds(i * n if isinstance(i, int) else pl.multiple_of(i * n, n), n)

    tok, cot, w_out, grad_out = r.tok, r.cot, r.w_out, r.grad_out
    loads = []

    def load(src, dst):
        one = pltpu.make_async_copy(src, dst, local.at[len(loads)])
        one.start()
        loads.append(one)
        return one

    t_load, c_load = load(tok_hbm, tok), load(cot_hbm, cot)

    barrier = pltpu.get_barrier_semaphore()
    peers = [at_x(d) for d in (1, 2, 3)] + [at_y(d) for d in (1, 2, 3)] + [at_z(d) for d in range(1, 8)] + [sib]
    for peer in peers:
        pl.semaphore_signal(barrier, inc=1, device_id=peer, device_id_type=MESH)
    pl.semaphore_wait(barrier, len(peers))

    t_load.wait()
    c_load.wait()
    t_in = send(tok, r.tok_sib, sem.inp, 0, sib)
    c_in = send(cot, r.cot_sib, sem.inp, 1, sib)

    def w_cols(block, x_):
        return span(block * 4 + x_, 384)

    w_loads = [load(w_in.at[:, w_cols(b, x)], w_mine.at[span(x, 192), span(b, 384)]) for b in range(2)]
    w_out_load = load(w_out_hbm, w_out)

    row = lax.broadcasted_iota(jnp.int32, (192, 384), 0)
    col = lax.broadcasted_iota(jnp.int32, (192, 384), 1)
    put_own = jnp.where(col == row + 192 * c, 1.0, 0.0).astype(bf16)
    put_sib = jnp.where(col == row + 192 * oc, 1.0, 0.0).astype(bf16)

    def chip(own, other):
        both = contract(own[...], put_own, 0, 0) + contract(other[...], put_sib, 0, 0)
        return both.astype(bf16).reshape(2, 4, 16, 384)

    recv(t_in)
    r.tok_chip[...] = chip(tok, r.tok_sib)

    half, l_mine = zl // 2, lax.rem(zl, 2)
    my16 = span(c * 2 + zh, 16)
    t_piece, t_place = r.tok_chip.at[c], tok_all.at[:, x, my16, span(l_mine, 384)]
    for j in (0, 1, 2, 3):
        send_unless(
            jnp.logical_and(half == zh, zl == j),
            copy(t_piece, t_place, sem.tz, (j,), dev(x, y, half * 4 + j, c), (zh * 2 + l_mine,)),
        )

    @pl.when(half == zh)
    def _():
        t_place[...] = t_piece[...]

    recv(c_in)
    r.cot_chip[...] = chip(cot, r.cot_sib)
    c_piece, c_place = r.cot_chip.at[c], cot_all.at[:, x, my16, span(zl, 384)]
    cx = [send(c_piece, c_place, sem.cx, (d - 1,), at_x(d)) for d in (2, 1, 3)]
    c_place[...] = c_piece[...]
    w_copies = [
        send(w_in.at[:, w_cols(b, mod(x, d, 4))], w_mine.at[span(x, 192), span(b, 384)], sem.w, (d - 1, b), at_x(d))
        for d in (2, 1, 3)
        for b in range(2)
    ]


    def c_flow():
        c_sib = []

        def block(d, k):
            z_ = mod(z, d + 8, 8)
            return cot_all.at[span(k, 2), :, span(c * 2 + z_ // 4, 16), span(lax.rem(z_, 4), 384)]

        def onward(d, k, way, s):
            return send(block(d, k), block(d, k), sem.cz, (way, s, k), at_z(1 if way == 0 else 7))

        def to_sib(d, k):
            c_sib.append(send(block(d, k), block(d, k), sem.csib, (d % 8, k), sib))

        recv(*cx)
        ring = {}
        for k in range(2):
            for way in range(2):
                ring[way, k] = onward(0, k, way, 0)
        for k in range(2):
            to_sib(0, k)
        yield
        for s in range(1, 4):
            for k in range(2):
                for way in range(2):
                    recv(ring[way, k])
                    d = -s if way == 0 else s
                    if s < 3 or k == way:
                        ring[way, k] = onward(d, k, way, s)
                    to_sib(d, k)
            yield
        for k in range(2):
            recv(ring[k, k])
            to_sib(4, k)
        yield
        recv(*c_sib)
        yield

    c_steps = c_flow()
    next(c_steps)

    for s in range(2):
        for l in range(2):
            recv_unless(
                jnp.logical_and(zh == s, zl == 2 * zh + l), copy(t_piece, t_place, sem.tz, (0,), sib, (s * 2 + l,))
            )

    def t_rows(d):
        return tok_all.at[:, mod(x, d, 4), span(c, 32)]

    tx = {d: send(t_rows(0), t_rows(0), sem.tx, (d - 1,), at_x(d)) for d in (1, 3, 2)}
    t_sib = {0: send(t_rows(0), t_rows(0), sem.tsib, (0,), sib)}

    def t_arrive(d):
        recv(tx[4 - d])
        t_sib[d] = send(t_rows(d), t_rows(d), sem.tsib, (d,), sib)

    steps_x = (0, 1, 3, 2)
    blocks = (oh, zh)
    fwd, direct, joined = {}, {}, {}

    def pre_block(i):
        d = steps_x[i]
        recv(t_sib[d])
        rows = tok_all[:, mod(x, d, 4)].reshape(256, 768)
        near, far = (1, 3) if i % 2 == 0 else (3, 1)
        for b in range(2):
            r.pre_part[b, i] = contract(rows, w_mine[:, span(blocks[b], 384)], 1, 0).reshape(4, 64, 384)
            for j, to in ((0, near), (1, far)):
                whose = 2 if j == 0 else far
                r.pre_send[b, i, j] = r.pre_part[b, i, mod(y, whose, 4)].astype(bf16)
                src = r.pre_send.at[b, i, j]
                if j == 0:
                    fwd[b, i] = send(src, r.pre_fwd.at[b, i], sem.pre, (b, i, 0), at_y(to))
                else:
                    direct[b, i] = send(src, r.pre_recv.at[b, i, 0], sem.pre, (b, i, 1), at_y(to))

    def pre_join(b, i):
        near = 1 if i % 2 == 0 else 3
        recv(fwd[b, i])
        r.pre_send[b, i, 2] = (r.pre_part[b, i, mod(y, near, 4)] + r.pre_fwd[b, i].astype(f32)).astype(bf16)
        joined[b, i] = send(r.pre_send.at[b, i, 2], r.pre_recv.at[b, i, 1], sem.pre, (b, i, 2), at_y(near))

    def pre_total(b, i):
        recv(direct[b, i], joined[b, i])
        return r.pre_part[b, i, y] + r.pre_recv[b, i, 0].astype(f32) + r.pre_recv[b, i, 1].astype(f32)

    across = {}

    def pre_across(i):
        r.half_send[i] = pre_total(0, i).astype(bf16)
        across[i] = send(r.half_send.at[i], r.half_recv.at[i], sem.half, (i,), at_z(4))

    next(c_steps)
    for one in w_loads:
        one.wait()
    recv(*w_copies)
    pre_block(0)
    next(c_steps)
    t_arrive(1)
    t_arrive(3)
    pre_block(1)
    pre_join(0, 0)
    pre_join(1, 0)
    pre_block(2)
    next(c_steps)
    t_arrive(2)
    pre_join(0, 1)
    pre_join(1, 1)
    pre_block(3)
    pre_across(0)
    pre_join(0, 2)
    pre_join(1, 2)
    pre_across(1)
    next(c_steps)
    pre_join(0, 3)
    pre_join(1, 3)
    pre_across(2)
    next(c_steps)

    low, high = span(0, 128), span(1, 128)
    back_part, back_send, back_recv, back_fwd = r.back_part, r.back_send, r.back_recv, r.back_fwd
    w_out_load.wait()
    for d in (2, 1, 3, 0):
        back_part[d] = contract(cot_all[mod(y, d, 4)].reshape(256, 1536), w_out[...], 1, 1)
        if d == 2:
            back_send[1] = back_part[2].astype(bf16)
            b_low = send(back_send.at[1, low], back_fwd.at[0], sem.back, (0,), at_y(1))
            b_high = send(back_send.at[1, high], back_fwd.at[1], sem.back, (1,), at_y(3))
        elif d == 1:
            back_send[0, high] = back_part[1, high].astype(bf16)
            b_direct = [send(back_send.at[0, high], back_recv.at[0, high], sem.back, (2,), at_y(1))]
        elif d == 3:
            back_send[2, low] = back_part[3, low].astype(bf16)
            b_direct.append(send(back_send.at[2, low], back_recv.at[1, low], sem.back, (3,), at_y(3)))
    pre_across(3)
    recv(b_low)
    back_send[0, low] = (back_part[1, low] + back_fwd[0].astype(f32)).astype(bf16)
    b_direct.append(send(back_send.at[0, low], back_recv.at[0, low], sem.back, (4,), at_y(1)))
    recv(b_high)
    back_send[2, high] = (back_part[3, high] + back_fwd[1].astype(f32)).astype(bf16)
    b_direct.append(send(back_send.at[2, high], back_recv.at[1, high], sem.back, (5,), at_y(3)))

    def y_gather(ref, cols, pair, lead):
        def place(d, rows=None):
            part = mod(y, d, 4)
            return ref.at[part, :, cols] if rows is None else ref.at[part, rows, cols]

        right = send(place(0), place(0), pair, lead + (0,), at_y(1))
        left = send(place(0), place(0), pair, lead + (1,), at_y(3))
        yield
        recv(right)
        on_right = send(place(3, low), place(3, low), pair, lead + (2,), at_y(1))
        recv(left)
        on_left = send(place(1, high), place(1, high), pair, lead + (3,), at_y(3))
        yield
        recv(on_right, on_left)
        yield

    for i in range(4):
        rows = span(mod(x, steps_x[i], 4), 64)
        own = pre_total(1, i)
        recv(across[i])
        h = own + r.half_recv[i].astype(f32)
        t = jnp.tanh(gelu_scale * (h + 0.044715 * h * h * h))
        act[y, rows, :] = (0.5 * h * (1.0 + t)).astype(bf16)
        r.slope[rows, :] = 0.5 * (1.0 + t) + 0.5 * h * (1.0 - t * t) * gelu_scale * (1.0 + 0.134145 * h * h)
    a_steps = y_gather(act, slice(None), sem.act, ())
    next(a_steps)
    recv(*b_direct)
    gph = []
    my_cols, other_cols = span(zh, 384), span(oh, 384)
    for i in range(4):
        rows = span(i, 64)
        total = back_part[0, rows] + back_recv[0, rows].astype(f32) + back_recv[1, rows].astype(f32)
        gp[y, rows, my_cols] = (total * r.slope[rows, :]).astype(bf16)
        place = gp.at[y, rows, my_cols]
        gph.append(send(place, place, sem.gph, (i,), at_z(4)))
    g_own = y_gather(gp, my_cols, sem.gp, (0,))
    next(g_own)

    def o_flow(d):
        q = mod(y, d, 4)
        part, own = r.o_part.at[d], r.o_own.at[d]
        part[...] = contract(act[q], w_out[...], 1, 0).reshape(4, 64, 1536)
        r.o_sib_send[d] = part[:, span(oc, 32), :].astype(bf16)
        swap = send(r.o_sib_send.at[d], r.o_sib_recv.at[d], sem.osib, (d,), sib)
        yield
        recv(swap)
        own[...] = part[:, span(c, 32), :] + r.o_sib_recv[d].astype(f32)

        def block(e):
            z_ = mod(z, e, 8)
            return own.at[:, span(z_ // 4, 16), span(lax.rem(z_, 4), 384)]

        halves = (pl.ds(0, 2), pl.ds(2, 2))
        ring = {}
        for step in range(4):
            for way in range(2):
                to_send, got = r.o_ring_send.at[d, way, step], r.o_ring_recv.at[d, way]
                e = 4 - step if way == 0 else 4 + step
                where = halves[way] if step == 0 else slice(None)
                if step:
                    recv(ring[way])
                if step == 0:
                    to_send[where] = block(e)[where].astype(bf16)
                elif step == 1:
                    with_, without = halves[way], halves[1 - way]
                    to_send[with_] = (block(e)[with_] + got[0, with_].astype(f32)).astype(bf16)
                    to_send[without] = block(e)[without].astype(bf16)
                else:
                    to_send[...] = (block(e)[...] + got[step - 1].astype(f32)).astype(bf16)
                ring[way] = send(
                    to_send.at[where], got.at[step, where], sem.oring, (d, way, step), at_z(1 if way == 0 else 7)
                )
            yield
        recv(ring[0], ring[1])
        got = r.o_ring_recv
        r.o_x_own[d] = block(0)[...] + got[d, 0, 3].astype(f32) + got[d, 1, 3].astype(f32)
        r.o_x_send[d] = r.o_x_own[d].astype(bf16)
        ox = [
            send(r.o_x_send.at[d, mod(x, e, 4)], r.o_x_recv.at[d, e - 1], sem.ox, (d, e - 1), at_x(e)) for e in (2, 1, 3)
        ]
        yield
        recv(*ox)
        total = r.o_x_own[d, x]
        for e in range(3):
            total = total + r.o_x_recv[d, e].astype(f32)
        r.o_fin[c, q] = total.astype(bf16)
        yield

    def g_flow(d):
        q = mod(y, d, 4)
        part, own = r.g_part.at[d], r.g_own.at[d]
        part[...] = contract(gp[q], w_mine[...], 1, 1).reshape(4, 64, 768)
        r.g_sib_send[d] = part[:, span(oc, 32), :].astype(bf16)
        swap = send(r.g_sib_send.at[d], r.g_sib_recv.at[d], sem.gsib, (d,), sib)
        yield
        recv(swap)
        own[...] = part[:, span(c, 32), :] + r.g_sib_recv[d].astype(f32)
        gx = []
        for e in (2, 1, 3):
            r.g_x_send[d, e - 1] = own[mod(x, e, 4)].astype(bf16)
            gx.append(send(r.g_x_send.at[d, e - 1], r.g_x_recv.at[d, e - 1], sem.gx, (d, e - 1), at_x(e)))
        yield
        recv(*gx)
        total = own[x]
        for e in range(3):
            total = total + r.g_x_recv[d, e].astype(f32)
        r.g_z_send[d] = total.astype(bf16)
        for s in range(2):
            for l in range(2):
                mine = jnp.logical_and(zh == s, zl == 2 * zh + l)
                piece = r.g_z_send.at[d, span(s, 16), span(l, 384)]
                send_unless(
                    mine, copy(piece, r.g_z_recv.at[d, zl], sem.gz, (d, s * 2 + l), dev(x, y, s * 4 + 2 * zh + l, c), (d, zl))
                )

                @pl.when(mine)
                def _():
                    r.g_z_recv[d, zl] = piece[...]

        yield
        for j in range(4):
            recv_unless(
                jnp.logical_and(half == zh, zl == j),
                copy(r.g_z_send.at[d, span(0, 16), span(0, 384)], r.g_z_recv.at[d, j], sem.gz, (d, 0), sib, (d, j)),
            )
        total = r.g_z_recv[d, 0].astype(f32)
        for j in range(1, 4):
            total = total + r.g_z_recv[d, j].astype(f32)
        r.g_fin[c, q] = total.astype(bf16)
        yield

    gi, gi_own = [], []

    def gi_flow():
        for b, which in enumerate((zh, oh)):
            for p in range(2):
                rows = span(p, 384)
                r.gi_send[rows, span(b, 384)] = contract(
                    tok_all[:, :, :, rows].reshape(1024, 384), gp[:, :, span(which, 384)].reshape(1024, 384), 0, 0
                ).astype(bf16)
            for d in (2, 1, 3):
                gi.append(
                    send(
                        r.gi_send.at[span(mod(x, d, 4), 192), span(b, 384)], grad_in.at[:, w_cols(which, x)],
                        sem.gi, (b, d - 1), at_x(d),
                    )
                )
            gi_own.append(load(r.gi_send.at[span(x, 192), span(b, 384)], grad_in.at[:, w_cols(which, x)]))
            yield

    def go_flow():
        for n in range(4):
            cols = span(n, 384)
            grad_out[:, cols] = contract(
                act[...].reshape(1024, 384), cot_all[:, :, :, cols].reshape(1024, 384), 0, 0
            ).astype(bf16)
            yield

    def other_flow():
        recv(*gph)
        yield from y_gather(gp, other_cols, sem.gp, (1,))

    o = {d: o_flow(d) for d in range(4)}
    g = {d: g_flow(d) for d in range(4)}
    o0, o1, o2, o3 = o[0], o[1], o[2], o[3]
    g0, g1, g2, g3 = g[0], g[1], g[2], g[3]
    a, mine, other, gi_steps, go = a_steps, g_own, other_flow(), gi_flow(), go_flow()
    for flow in (o0, o0, a, o1, o1, mine, o3, o3, o0, other, g0, a, mine, gi_steps, g0, o2, o2, o0, o1, o3, other, g1, g3, g1, g3, o0, o1, o2, other, g2, g2, gi_steps, g0, o0, o1, o3, g1, g3, o2, o3, go, g2, o1, o2, go, o3, o0, g0, g1, g3, o2, go):
        next(flow)
    for flow in (g0, g1, g3, g2):
        for _ in flow:
            pass
    g_last = send(r.g_fin.at[c], r.g_fin.at[c], sem.gfin, (0,), sib)
    for flow in (o0, o1, o3, o2):
        for _ in flow:
            pass
    o_last = send(r.o_fin.at[c], r.o_fin.at[c], sem.ofin, (0,), sib)
    for _ in go:
        pass
    stored = load(grad_out, grad_out_hbm)

    row = lax.broadcasted_iota(jnp.int32, (384, 192), 0)
    col = lax.broadcasted_iota(jnp.int32, (384, 192), 1)
    take = jnp.where(row == col + 192 * c, 1.0, 0.0).astype(bf16)
    recv(o_last)
    out[...] = contract(take, r.o_fin[...].reshape(128, 384), 0, 1).astype(bf16)
    recv(g_last)
    grad_tok[...] = contract(take, r.g_fin[...].reshape(128, 384), 0, 1).astype(bf16)
    recv(*gi)
    stored.wait()
    for one in gi_own:
        one.wait()
    assert not coming
    for one in started:
        one.wait_send()
    for mine, one in maybe:

        @pl.when(jnp.logical_not(mine))
        def _():
            one.wait_send()


def hand_over(*refs):
    loads = [pltpu.make_async_copy(refs[i], refs[8 + i], refs[12].at[i]) for i in range(4)]
    stores = [pltpu.make_async_copy(refs[8 + i], refs[4 + i], refs[12].at[4 + i]) for i in range(4)]
    for one in loads:
        one.start()
    for one, then in zip(loads, stores):
        one.wait()
        then.start()
    for one in stores:
        one.wait()


def on_device(tokens, w_in, w_out, cotangent):
    scratch = [pltpu.VMEM(dims, dtype) for dims, dtype in buffers().values()]
    for dims in semaphores().values():
        scratch += [pltpu.SemaphoreType.DMA(dims)] * 2
    scratch.append(pltpu.SemaphoreType.DMA((8,)))
    shape = jax.ShapeDtypeStruct
    vmem, hbm = pl.BlockSpec(memory_space=pltpu.VMEM), pl.BlockSpec(memory_space=pl.ANY)
    shapes = (shape((192, 128), bf16), shape((192, 128), bf16), shape((192, 3072), bf16), shape((384, 1536), bf16))
    results = pl.pallas_call(
        kernel,
        out_shape=shapes,
        in_specs=[hbm] * 4,
        out_specs=[vmem, vmem, hbm, hbm],
        scratch_shapes=scratch,
        compiler_params=pltpu.CompilerParams(
            collective_id=0, has_side_effects=True, vmem_limit_bytes=60 * 1024 * 1024
        ),
        cost_estimate=pl.CostEstimate(flops=7_250_000_000, bytes_accessed=5_000_000, transcendentals=100_000),
    )(tokens.T, w_in, w_out, cotangent.T)
    out, grad_tokens, grad_in, grad_out = pl.pallas_call(
        hand_over,
        out_shape=shapes,
        in_specs=[hbm] * 4,
        out_specs=[hbm] * 4,
        scratch_shapes=[pltpu.VMEM(one.shape, one.dtype) for one in shapes] + [pltpu.SemaphoreType.DMA((8,))],
    )(*results)
    return out.T, grad_tokens.T, grad_in, grad_out


def solution(mesh):
    specs = (P("gx", ("gz", "gy")), P(("gz", "gx"), "gy"), P(("gy", "gx"), "gz"))
    return jax.shard_map(
        on_device,
        mesh=mesh,
        in_specs=(specs[0], specs[1], specs[2], specs[0]),
        out_specs=(specs[0], specs[0], specs[1], specs[2]),
        check_vma=False,
    )
```

```python
import types

import jax
import jax.numpy as jnp
from jax import lax
from jax.experimental import pallas as pl
from jax.experimental.pallas import tpu as pltpu
from jax.sharding import PartitionSpec as P

MESH = pl.DeviceIdType.MESH
gelu_scale = 0.7978845608
bf16, f32 = jnp.bfloat16, jnp.float32


def contract(left, right, left_dim, right_dim):
    return lax.dot_general(
        left, right, (((left_dim,), (right_dim,)), ((), ())), preferred_element_type=f32
    )


def buffers():
    return dict(
        tok=((192, 128), bf16), cot=((192, 128), bf16), w_out=((384, 1536), bf16), grad_out=((384, 1536), bf16),
        tok_sib=((192, 128), bf16), cot_sib=((192, 128), bf16),
        tok_chip=((2, 4, 16, 384), bf16), cot_chip=((2, 4, 16, 384), bf16),
        tok_all=((4, 4, 64, 768), bf16), cot_all=((4, 4, 64, 1536), bf16), w_mine=((768, 768), bf16),
        pre_part=((2, 4, 4, 64, 384), f32), pre_send=((2, 4, 3, 64, 384), bf16),
        pre_fwd=((2, 4, 64, 384), bf16), pre_recv=((2, 4, 2, 64, 384), bf16),
        half_send=((4, 64, 384), bf16), half_recv=((4, 64, 384), bf16),
        back_part=((4, 256, 384), f32), back_send=((3, 256, 384), bf16),
        back_fwd=((2, 128, 384), bf16), back_recv=((2, 256, 384), bf16), slope=((256, 384), f32),
        act=((4, 256, 384), bf16), gp=((4, 256, 768), bf16),
        o_part=((4, 4, 64, 1536), f32), o_sib_send=((4, 4, 32, 1536), bf16), o_sib_recv=((4, 4, 32, 1536), bf16),
        o_own=((4, 4, 32, 1536), f32), o_ring_send=((4, 2, 4, 4, 16, 384), bf16), o_ring_recv=((4, 2, 4, 4, 16, 384), bf16),
        o_x_send=((4, 4, 16, 384), bf16), o_x_recv=((4, 3, 16, 384), bf16), o_x_own=((4, 4, 16, 384), f32),
        o_fin=((2, 4, 16, 384), bf16),
        g_part=((4, 4, 64, 768), f32), g_sib_send=((4, 4, 32, 768), bf16), g_sib_recv=((4, 4, 32, 768), bf16),
        g_own=((4, 4, 32, 768), f32), g_x_send=((4, 3, 32, 768), bf16), g_x_recv=((4, 3, 32, 768), bf16),
        g_z_send=((4, 32, 768), bf16), g_z_recv=((4, 4, 16, 384), bf16),
        g_fin=((2, 4, 16, 384), bf16), gi_send=((768, 768), bf16),
    )


def semaphores():
    return dict(
        inp=(2,), w=(3, 2), tz=(4,), cx=(3,), cz=(2, 4, 2), csib=(8, 2), tx=(3,), tsib=(4,),
        pre=(2, 4, 3), half=(4,), back=(6,), act=(4,), gp=(2, 4), gph=(4,),
        osib=(4,), oring=(4, 2, 4), ox=(4, 3), ofin=(1,),
        gsib=(4,), gx=(4, 3), gz=(4, 4), gfin=(1,), gi=(2, 3),
    )


def kernel(*refs):
    tok_hbm, w_in, w_out_hbm, cot_hbm, out, grad_tok, grad_in, grad_out_hbm = refs[:8]
    bufs = buffers()
    r = types.SimpleNamespace(**dict(zip(bufs, refs[8:])))
    rest = refs[8 + len(bufs):]
    local = rest[-1]
    sem = types.SimpleNamespace(**{name: rest[2 * i : 2 * i + 2] for i, name in enumerate(semaphores())})
    tok_all, cot_all, w_mine, act, gp = r.tok_all, r.cot_all, r.w_mine, r.act, r.gp

    ax, ay, y = lax.axis_index("gx"), lax.axis_index("gy"), lax.axis_index("gz")
    zh, x = ax // 4, lax.rem(ax, 4)
    zl, c = ay // 2, lax.rem(ay, 2)
    z = zh * 4 + zl
    oc, oh = 1 - c, 1 - zh

    def dev(x_, y_, z_, c_):
        return (z_ // 4 * 4 + x_, lax.rem(z_, 4) * 2 + c_, y_)

    def mod(v, d, n):
        return lax.rem(v + d, n)

    def at_x(d):
        return dev(mod(x, d, 4), y, z, c)

    def at_y(d):
        return dev(x, mod(y, d, 4), z, c)

    def at_z(d):
        return dev(x, y, mod(z, d, 8), c)

    sib = dev(x, y, z, oc)
    started, coming, maybe = [], [], []

    def copy(src, dst, pair, index, to, from_index=None):
        ss, rs = pair
        return pltpu.make_async_remote_copy(
            src_ref=src, dst_ref=dst, send_sem=ss.at[index], recv_sem=rs.at[index if from_index is None else from_index],
            device_id=to, device_id_type=MESH,
        )

    def send(src, dst, pair, index, to):
        one = copy(src, dst, pair, index, to)
        one.start()
        started.append(one)
        coming.append(one)
        return one

    def recv(*copies):
        for one in copies:
            one.wait_recv()
            coming[:] = [other for other in coming if other is not one]

    def send_unless(mine, one):
        maybe.append((mine, one))

        @pl.when(jnp.logical_not(mine))
        def _():
            one.start()

    def recv_unless(mine, one):
        @pl.when(jnp.logical_not(mine))
        def _():
            one.wait_recv()

    def span(i, n):
        return pl.ds(i * n if isinstance(i, int) else pl.multiple_of(i * n, n), n)

    tok, cot, w_out, grad_out = r.tok, r.cot, r.w_out, r.grad_out
    loads = []

    def load(src, dst):
        one = pltpu.make_async_copy(src, dst, local.at[len(loads)])
        one.start()
        loads.append(one)
        return one

    t_load, c_load = load(tok_hbm, tok), load(cot_hbm, cot)

    barrier = pltpu.get_barrier_semaphore()
    peers = [at_x(d) for d in (1, 2, 3)] + [at_y(d) for d in (1, 2, 3)] + [at_z(d) for d in range(1, 8)] + [sib]
    for peer in peers:
        pl.semaphore_signal(barrier, inc=1, device_id=peer, device_id_type=MESH)
    t_load.wait()
    c_load.wait()
    row = lax.broadcasted_iota(jnp.int32, (192, 384), 0)
    col = lax.broadcasted_iota(jnp.int32, (192, 384), 1)
    put_own = jnp.where(col == row + 192 * c, 1.0, 0.0).astype(bf16)
    put_sib = jnp.where(col == row + 192 * oc, 1.0, 0.0).astype(bf16)
    t_own = contract(tok[...], put_own, 0, 0)
    c_own = contract(cot[...], put_own, 0, 0)
    pl.semaphore_wait(barrier, len(peers))

    t_in = send(tok, r.tok_sib, sem.inp, 0, sib)
    c_in = send(cot, r.cot_sib, sem.inp, 1, sib)

    def w_cols(block, x_):
        return span(block * 4 + x_, 384)

    w_loads = [load(w_in.at[:, w_cols(b, x)], w_mine.at[span(x, 192), span(b, 384)]) for b in range(2)]
    w_out_load = load(w_out_hbm, w_out)

    def chip(own, other):
        both = own + contract(other[...], put_sib, 0, 0)
        return both.astype(bf16).reshape(2, 4, 16, 384)

    recv(t_in)
    r.tok_chip[...] = chip(t_own, r.tok_sib)

    half, l_mine = zl // 2, lax.rem(zl, 2)
    my16 = span(c * 2 + zh, 16)
    t_piece, t_place = r.tok_chip.at[c], tok_all.at[:, x, my16, span(l_mine, 384)]
    for j in (0, 1, 2, 3):
        send_unless(
            jnp.logical_and(half == zh, zl == j),
            copy(t_piece, t_place, sem.tz, (j,), dev(x, y, half * 4 + j, c), (zh * 2 + l_mine,)),
        )

    @pl.when(half == zh)
    def _():
        t_place[...] = t_piece[...]

    recv(c_in)
    r.cot_chip[...] = chip(c_own, r.cot_sib)
    c_piece, c_place = r.cot_chip.at[c], cot_all.at[:, x, my16, span(zl, 384)]
    cx = [send(c_piece, c_place, sem.cx, (d - 1,), at_x(d)) for d in (2, 1, 3)]
    c_place[...] = c_piece[...]
    w_copies = [
        send(w_in.at[:, w_cols(b, mod(x, d, 4))], w_mine.at[span(x, 192), span(b, 384)], sem.w, (d - 1, b), at_x(d))
        for d in (2, 1, 3)
        for b in range(2)
    ]


    def c_flow():
        c_sib = []

        def block(d, k):
            z_ = mod(z, d + 8, 8)
            return cot_all.at[span(k, 2), :, span(c * 2 + z_ // 4, 16), span(lax.rem(z_, 4), 384)]

        def onward(d, k, way, s):
            return send(block(d, k), block(d, k), sem.cz, (way, s, k), at_z(1 if way == 0 else 7))

        def to_sib(d, k):
            c_sib.append(send(block(d, k), block(d, k), sem.csib, (d % 8, k), sib))

        recv(*cx)
        ring = {}
        for k in range(2):
            for way in range(2):
                ring[way, k] = onward(0, k, way, 0)
        for k in range(2):
            to_sib(0, k)
        yield
        for s in range(1, 4):
            for k in range(2):
                for way in range(2):
                    recv(ring[way, k])
                    d = -s if way == 0 else s
                    if s < 3 or k == way:
                        ring[way, k] = onward(d, k, way, s)
                    to_sib(d, k)
            yield
        for k in range(2):
            recv(ring[k, k])
            to_sib(4, k)
        yield
        recv(*c_sib)
        yield

    c_steps = c_flow()
    next(c_steps)

    for s in range(2):
        for l in range(2):
            recv_unless(
                jnp.logical_and(zh == s, zl == 2 * zh + l), copy(t_piece, t_place, sem.tz, (0,), sib, (s * 2 + l,))
            )

    def t_rows(d):
        return tok_all.at[:, mod(x, d, 4), span(c, 32)]

    tx = {d: send(t_rows(0), t_rows(0), sem.tx, (d - 1,), at_x(d)) for d in (1, 3, 2)}
    t_sib = {0: send(t_rows(0), t_rows(0), sem.tsib, (0,), sib)}

    def t_arrive(d):
        recv(tx[4 - d])
        t_sib[d] = send(t_rows(d), t_rows(d), sem.tsib, (d,), sib)

    steps_x = (0, 1, 3, 2)
    blocks = (oh, zh)
    fwd, direct, joined = {}, {}, {}

    def pre_block(i):
        d = steps_x[i]
        recv(t_sib[d])
        rows = tok_all[:, mod(x, d, 4)].reshape(256, 768)
        near, far = (1, 3) if i % 2 == 0 else (3, 1)
        for b in range(2):
            r.pre_part[b, i] = contract(rows, w_mine[:, span(blocks[b], 384)], 1, 0).reshape(4, 64, 384)
            for j, to in ((0, near), (1, far)):
                whose = 2 if j == 0 else far
                r.pre_send[b, i, j] = r.pre_part[b, i, mod(y, whose, 4)].astype(bf16)
                src = r.pre_send.at[b, i, j]
                if j == 0:
                    fwd[b, i] = send(src, r.pre_fwd.at[b, i], sem.pre, (b, i, 0), at_y(to))
                else:
                    direct[b, i] = send(src, r.pre_recv.at[b, i, 0], sem.pre, (b, i, 1), at_y(to))

    def pre_join(b, i):
        near = 1 if i % 2 == 0 else 3
        recv(fwd[b, i])
        r.pre_send[b, i, 2] = (r.pre_part[b, i, mod(y, near, 4)] + r.pre_fwd[b, i].astype(f32)).astype(bf16)
        joined[b, i] = send(r.pre_send.at[b, i, 2], r.pre_recv.at[b, i, 1], sem.pre, (b, i, 2), at_y(near))

    def pre_total(b, i):
        recv(direct[b, i], joined[b, i])
        return r.pre_part[b, i, y] + r.pre_recv[b, i, 0].astype(f32) + r.pre_recv[b, i, 1].astype(f32)

    across = {}

    def pre_across(i):
        r.half_send[i] = pre_total(0, i).astype(bf16)
        across[i] = send(r.half_send.at[i], r.half_recv.at[i], sem.half, (i,), at_z(4))

    next(c_steps)
    for one in w_loads:
        one.wait()
    recv(*w_copies)
    pre_block(0)
    next(c_steps)
    t_arrive(1)
    t_arrive(3)
    pre_block(1)
    pre_join(0, 0)
    pre_join(1, 0)
    pre_block(2)
    next(c_steps)
    t_arrive(2)
    pre_join(0, 1)
    pre_join(1, 1)
    pre_block(3)
    pre_across(0)
    pre_join(0, 2)
    pre_join(1, 2)
    pre_across(1)
    next(c_steps)
    pre_join(0, 3)
    pre_join(1, 3)
    pre_across(2)
    next(c_steps)

    low, high = span(0, 128), span(1, 128)
    back_part, back_send, back_recv, back_fwd = r.back_part, r.back_send, r.back_recv, r.back_fwd
    w_out_load.wait()
    for d in (2, 1, 3, 0):
        back_part[d] = contract(cot_all[mod(y, d, 4)].reshape(256, 1536), w_out[...], 1, 1)
        if d == 2:
            back_send[1] = back_part[2].astype(bf16)
            b_low = send(back_send.at[1, low], back_fwd.at[0], sem.back, (0,), at_y(1))
            b_high = send(back_send.at[1, high], back_fwd.at[1], sem.back, (1,), at_y(3))
        elif d == 1:
            back_send[0, high] = back_part[1, high].astype(bf16)
            b_direct = [send(back_send.at[0, high], back_recv.at[0, high], sem.back, (2,), at_y(1))]
        elif d == 3:
            back_send[2, low] = back_part[3, low].astype(bf16)
            b_direct.append(send(back_send.at[2, low], back_recv.at[1, low], sem.back, (3,), at_y(3)))
    pre_across(3)
    recv(b_low)
    back_send[0, low] = (back_part[1, low] + back_fwd[0].astype(f32)).astype(bf16)
    b_direct.append(send(back_send.at[0, low], back_recv.at[0, low], sem.back, (4,), at_y(1)))
    recv(b_high)
    back_send[2, high] = (back_part[3, high] + back_fwd[1].astype(f32)).astype(bf16)
    b_direct.append(send(back_send.at[2, high], back_recv.at[1, high], sem.back, (5,), at_y(3)))

    def y_gather(ref, cols, pair, lead):
        def place(d, rows=None):
            part = mod(y, d, 4)
            return ref.at[part, :, cols] if rows is None else ref.at[part, rows, cols]

        right = send(place(0), place(0), pair, lead + (0,), at_y(1))
        left = send(place(0), place(0), pair, lead + (1,), at_y(3))
        yield
        recv(right)
        on_right = send(place(3, low), place(3, low), pair, lead + (2,), at_y(1))
        recv(left)
        on_left = send(place(1, high), place(1, high), pair, lead + (3,), at_y(3))
        yield
        recv(on_right, on_left)
        yield

    for i in range(4):
        rows = span(mod(x, steps_x[i], 4), 64)
        own = pre_total(1, i)
        recv(across[i])
        h = own + r.half_recv[i].astype(f32)
        t = jnp.tanh(gelu_scale * (h + 0.044715 * h * h * h))
        act[y, rows, :] = (0.5 * h * (1.0 + t)).astype(bf16)
        r.slope[rows, :] = 0.5 * (1.0 + t) + 0.5 * h * (1.0 - t * t) * gelu_scale * (1.0 + 0.134145 * h * h)
    a_steps = y_gather(act, slice(None), sem.act, ())
    next(a_steps)
    recv(*b_direct)
    gph = []
    my_cols, other_cols = span(zh, 384), span(oh, 384)
    for i in range(4):
        rows = span(i, 64)
        total = back_part[0, rows] + back_recv[0, rows].astype(f32) + back_recv[1, rows].astype(f32)
        gp[y, rows, my_cols] = (total * r.slope[rows, :]).astype(bf16)
        place = gp.at[y, rows, my_cols]
        gph.append(send(place, place, sem.gph, (i,), at_z(4)))
    g_own = y_gather(gp, my_cols, sem.gp, (0,))
    next(g_own)

    def o_flow(d):
        q = mod(y, d, 4)
        part, own = r.o_part.at[d], r.o_own.at[d]
        part[...] = contract(act[q], w_out[...], 1, 0).reshape(4, 64, 1536)
        r.o_sib_send[d] = part[:, span(oc, 32), :].astype(bf16)
        swap = send(r.o_sib_send.at[d], r.o_sib_recv.at[d], sem.osib, (d,), sib)
        yield
        recv(swap)
        own[...] = part[:, span(c, 32), :] + r.o_sib_recv[d].astype(f32)

        def block(e):
            z_ = mod(z, e, 8)
            return own.at[:, span(z_ // 4, 16), span(lax.rem(z_, 4), 384)]

        halves = (pl.ds(0, 2), pl.ds(2, 2))
        ring = {}
        for step in range(4):
            for way in range(2):
                to_send, got = r.o_ring_send.at[d, way, step], r.o_ring_recv.at[d, way]
                e = 4 - step if way == 0 else 4 + step
                where = halves[way] if step == 0 else slice(None)
                if step:
                    recv(ring[way])
                if step == 0:
                    to_send[where] = block(e)[where].astype(bf16)
                elif step == 1:
                    with_, without = halves[way], halves[1 - way]
                    to_send[with_] = (block(e)[with_] + got[0, with_].astype(f32)).astype(bf16)
                    to_send[without] = block(e)[without].astype(bf16)
                else:
                    to_send[...] = (block(e)[...] + got[step - 1].astype(f32)).astype(bf16)
                ring[way] = send(
                    to_send.at[where], got.at[step, where], sem.oring, (d, way, step), at_z(1 if way == 0 else 7)
                )
            yield
        recv(ring[0], ring[1])
        got = r.o_ring_recv
        r.o_x_own[d] = block(0)[...] + got[d, 0, 3].astype(f32) + got[d, 1, 3].astype(f32)
        r.o_x_send[d] = r.o_x_own[d].astype(bf16)
        ox = [
            send(r.o_x_send.at[d, mod(x, e, 4)], r.o_x_recv.at[d, e - 1], sem.ox, (d, e - 1), at_x(e)) for e in (2, 1, 3)
        ]
        yield
        recv(*ox)
        total = r.o_x_own[d, x]
        for e in range(3):
            total = total + r.o_x_recv[d, e].astype(f32)
        r.o_fin[c, q] = total.astype(bf16)
        yield

    def g_flow(d):
        q = mod(y, d, 4)
        part, own = r.g_part.at[d], r.g_own.at[d]
        part[...] = contract(gp[q], w_mine[...], 1, 1).reshape(4, 64, 768)
        r.g_sib_send[d] = part[:, span(oc, 32), :].astype(bf16)
        swap = send(r.g_sib_send.at[d], r.g_sib_recv.at[d], sem.gsib, (d,), sib)
        yield
        recv(swap)
        own[...] = part[:, span(c, 32), :] + r.g_sib_recv[d].astype(f32)
        gx = []
        for e in (2, 1, 3):
            r.g_x_send[d, e - 1] = own[mod(x, e, 4)].astype(bf16)
            gx.append(send(r.g_x_send.at[d, e - 1], r.g_x_recv.at[d, e - 1], sem.gx, (d, e - 1), at_x(e)))
        yield
        recv(*gx)
        total = own[x]
        for e in range(3):
            total = total + r.g_x_recv[d, e].astype(f32)
        r.g_z_send[d] = total.astype(bf16)
        for s in range(2):
            for l in range(2):
                mine = jnp.logical_and(zh == s, zl == 2 * zh + l)
                piece = r.g_z_send.at[d, span(s, 16), span(l, 384)]
                send_unless(
                    mine, copy(piece, r.g_z_recv.at[d, zl], sem.gz, (d, s * 2 + l), dev(x, y, s * 4 + 2 * zh + l, c), (d, zl))
                )

                @pl.when(mine)
                def _():
                    r.g_z_recv[d, zl] = piece[...]

        yield
        for j in range(4):
            recv_unless(
                jnp.logical_and(half == zh, zl == j),
                copy(r.g_z_send.at[d, span(0, 16), span(0, 384)], r.g_z_recv.at[d, j], sem.gz, (d, 0), sib, (d, j)),
            )
        total = r.g_z_recv[d, 0].astype(f32)
        for j in range(1, 4):
            total = total + r.g_z_recv[d, j].astype(f32)
        r.g_fin[c, q] = total.astype(bf16)
        yield

    gi, gi_own = [], []

    def gi_flow():
        for b, which in enumerate((zh, oh)):
            for p in range(2):
                rows = span(p, 384)
                r.gi_send[rows, span(b, 384)] = contract(
                    tok_all[:, :, :, rows].reshape(1024, 384), gp[:, :, span(which, 384)].reshape(1024, 384), 0, 0
                ).astype(bf16)
            for d in (2, 1, 3):
                gi.append(
                    send(
                        r.gi_send.at[span(mod(x, d, 4), 192), span(b, 384)], grad_in.at[:, w_cols(which, x)],
                        sem.gi, (b, d - 1), at_x(d),
                    )
                )
            gi_own.append(load(r.gi_send.at[span(x, 192), span(b, 384)], grad_in.at[:, w_cols(which, x)]))
            yield

    def go_flow():
        for n in range(4):
            cols = span(n, 384)
            grad_out[:, cols] = contract(
                act[...].reshape(1024, 384), cot_all[:, :, :, cols].reshape(1024, 384), 0, 0
            ).astype(bf16)
            yield

    def other_flow():
        recv(*gph)
        yield from y_gather(gp, other_cols, sem.gp, (1,))

    o = {d: o_flow(d) for d in range(4)}
    g = {d: g_flow(d) for d in range(4)}
    o0, o1, o2, o3 = o[0], o[1], o[2], o[3]
    g0, g1, g2, g3 = g[0], g[1], g[2], g[3]
    a, mine, other, gi_steps, go = a_steps, g_own, other_flow(), gi_flow(), go_flow()
    for flow in (o0, o0, a, o1, o1, mine, o3, o3, o0, other, g0, a, mine, gi_steps, g0, o2, o2, o0, o1, o3, other, g1, g3, g1, g3, o0, o1, o2, other, g2, g2, gi_steps, g0, o0, o1, o3, g1, g3, o2, o3, go, g2, o1, o2, go, o3, o0, g0, g1, g3, o2, go):
        next(flow)
    for flow in (g0, g1, g3, g2):
        for _ in flow:
            pass
    g_last = send(r.g_fin.at[c], r.g_fin.at[c], sem.gfin, (0,), sib)
    for flow in (o0, o1, o3, o2):
        for _ in flow:
            pass
    o_last = send(r.o_fin.at[c], r.o_fin.at[c], sem.ofin, (0,), sib)
    for _ in go:
        pass
    stored = load(grad_out, grad_out_hbm)

    row = lax.broadcasted_iota(jnp.int32, (384, 192), 0)
    col = lax.broadcasted_iota(jnp.int32, (384, 192), 1)
    take = jnp.where(row == col + 192 * c, 1.0, 0.0).astype(bf16)
    recv(o_last)
    out[...] = contract(take, r.o_fin[...].reshape(128, 384), 0, 1).astype(bf16)
    recv(g_last)
    grad_tok[...] = contract(take, r.g_fin[...].reshape(128, 384), 0, 1).astype(bf16)
    recv(*gi)
    stored.wait()
    for one in gi_own:
        one.wait()
    assert not coming
    for one in started:
        one.wait_send()
    for mine, one in maybe:

        @pl.when(jnp.logical_not(mine))
        def _():
            one.wait_send()


def hand_over(*refs):
    loads = [pltpu.make_async_copy(refs[i], refs[8 + i], refs[12].at[i]) for i in range(4)]
    stores = [pltpu.make_async_copy(refs[8 + i], refs[4 + i], refs[12].at[4 + i]) for i in range(4)]
    for one in loads:
        one.start()
    for one, then in zip(loads, stores):
        one.wait()
        then.start()
    for one in stores:
        one.wait()


def on_device(tokens, w_in, w_out, cotangent):
    scratch = [pltpu.VMEM(dims, dtype) for dims, dtype in buffers().values()]
    for dims in semaphores().values():
        scratch += [pltpu.SemaphoreType.DMA(dims)] * 2
    scratch.append(pltpu.SemaphoreType.DMA((8,)))
    shape = jax.ShapeDtypeStruct
    vmem, hbm = pl.BlockSpec(memory_space=pltpu.VMEM), pl.BlockSpec(memory_space=pl.ANY)
    shapes = (shape((192, 128), bf16), shape((192, 128), bf16), shape((192, 3072), bf16), shape((384, 1536), bf16))
    results = pl.pallas_call(
        kernel,
        out_shape=shapes,
        in_specs=[hbm] * 4,
        out_specs=[vmem, vmem, hbm, hbm],
        scratch_shapes=scratch,
        compiler_params=pltpu.CompilerParams(
            collective_id=0, has_side_effects=True, vmem_limit_bytes=60 * 1024 * 1024
        ),
        cost_estimate=pl.CostEstimate(flops=7_250_000_000, bytes_accessed=5_000_000, transcendentals=100_000),
    )(tokens.T, w_in, w_out, cotangent.T)
    out, grad_tokens, grad_in, grad_out = pl.pallas_call(
        hand_over,
        out_shape=shapes,
        in_specs=[hbm] * 4,
        out_specs=[hbm] * 4,
        scratch_shapes=[pltpu.VMEM(one.shape, one.dtype) for one in shapes] + [pltpu.SemaphoreType.DMA((8,))],
    )(*results)
    return out.T, grad_tokens.T, grad_in, grad_out


def solution(mesh):
    specs = (P("gx", ("gz", "gy")), P(("gz", "gx"), "gy"), P(("gy", "gx"), "gz"))
    return jax.shard_map(
        on_device,
        mesh=mesh,
        in_specs=(specs[0], specs[1], specs[2], specs[0]),
        out_specs=(specs[0], specs[0], specs[1], specs[2]),
        check_vma=False,
    )
```
